32 devices in a mesh: dp: 16 (over z, y, core), mp: 2 (over x).
Axes of the slice: x: 2, y: 2, z: 4, core: 2. Of those that a mesh axis runs over, the one named last changes fastest.
Arguments:
- inputs: float32 [128, 384, 384], P('dp'), may hold values from -6 to 6
- out_grad: float32 [128, 384, 384], P('dp'), may hold values from -6 to 6
- counts: int32 [128], P('dp'), may hold values from 32 to 128, as said below
- qkv_weight: float32 [3, 384, 384], P(None, 'dp', 'mp'), may hold values from -0.3125 to 0.3125
- out_weight: float32 [384, 384], P('mp', 'dp'), may hold values from -3 to 3
- up_weight: float32 [384, 1536], P('dp', 'mp'), may hold values from -0.3125 to 0.3125
- down_weight: float32 [1536, 384], P('mp', 'dp'), may hold values from -0.15625 to 0.15625
- norm_vectors: float32 [2, 384], P(None, 'dp'), may hold values from 0.55 to 1.45, as said below
- qkv_first: float32 [3, 384, 384], P(None, 'dp', 'mp'), may hold values from -640 to 640
- out_first: float32 [384, 384], P('mp', 'dp'), may hold values from -128 to 128
- up_first: float32 [384, 1536], P('dp', 'mp'), may hold values from -384 to 384
- down_first: float32 [1536, 384], P('mp', 'dp'), may hold values from -640 to 640
- norm_first: float32 [2, 384], P(None, 'dp'), may hold values from -640 to 640
- qkv_second: float32 [3, 384, 384], P(None, 'dp', 'mp'), may hold values from 12288 to 49152
- out_second: float32 [384, 384], P('mp', 'dp'), may hold values from 491.52 to 1966.08
- up_second: float32 [384, 1536], P('dp', 'mp'), may hold values from 4423.68 to 17694.72
- down_second: float32 [1536, 384], P('mp', 'dp'), may hold values from 12288 to 49152
- norm_second: float32 [2, 384], P(None, 'dp'), may hold values from 12288 to 49152
Outputs:
- block_out: float32 [128, 384, 384], P('dp')
- input_grad: float32 [128, 384, 384], P('dp')
- qkv_new: float32 [3, 384, 384], P(None, 'dp', 'mp')
- out_new: float32 [384, 384], P('mp', 'dp')
- up_new: float32 [384, 1536], P('dp', 'mp')
- down_new: float32 [1536, 384], P('mp', 'dp')
- norm_vectors_updated: float32 [2, 384], P(None, 'dp')
- qkv_first_new: float32 [3, 384, 384], P(None, 'dp', 'mp')
- out_first_new: float32 [384, 384], P('mp', 'dp')
- up_first_new: float32 [384, 1536], P('dp', 'mp')
- down_first_new: float32 [1536, 384], P('mp', 'dp')
- norm_first_new: float32 [2, 384], P(None, 'dp')
- qkv_second_new: float32 [3, 384, 384], P(None, 'dp', 'mp')
- out_second_new: float32 [384, 384], P('mp', 'dp')
- up_second_new: float32 [384, 1536], P('dp', 'mp')
- down_second_new: float32 [1536, 384], P('mp', 'dp')
- norm_second_new: float32 [2, 384], P(None, 'dp')
- qkv_grad_sum: float32 [3, 384, 384], P(None, 'dp', 'mp')
- out_grad_sum: float32 [384, 384], P('mp', 'dp')
- up_grad_sum: float32 [384, 1536], P('dp', 'mp')
- down_grad_sum: float32 [1536, 384], P('mp', 'dp')
- norm_grad_sum: float32 [2, 384], P(None, 'dp')
The draws below stay inside these ranges and needn't reach their ends.
Inputs may be any that keep to these rules, and one draw needn't show every extreme that they name: `counts`: each image's count is a quarter, a half or all of 128; every draw holds both a full and a quarter count. `norm_vectors`: both rows are gains near one.
All inputs are finite; a program needn't handle non-finite values.
Results may differ from the reference program's by a relative error of at most 0.013.
The reference program's roundings to bfloat16 on the way count: a program that leaves them out, or rounds other values in their place, can miss the bound.
Values may be sent and summed in bfloat16 or wider, within the bound.
A program may use at most 128 MiB of HBM per device.

```python
import math
import jax
import jax.numpy as jnp
from jax import lax

D = 384
HEADS = 6
HEAD_DIM = 64
FF = 1536
LATENTS = 128
PATCHES = 256
STEP = 5
SEQ = 384
IMAGES = 128
TOKENS = 49152


def draw_counts(key, part):
    key = jax.random.fold_in(key, 11)
    level_key, position_key = jax.random.split(key)
    levels = jax.random.randint(level_key, (IMAGES,), 0, 3)
    level_table = jnp.array([LATENTS // 4, LATENTS // 2, LATENTS], jnp.int32)
    counts = jnp.take(level_table, levels)
    position = jax.random.randint(position_key, (), 0, IMAGES)
    counts = counts.at[position].set(LATENTS)
    counts = counts.at[(position + 1) % IMAGES].set(LATENTS // 4)
    return counts.astype(jnp.int32)


def draw_norm_vectors(key, part):
    key = jax.random.fold_in(key, 23)
    normal_draw = jnp.clip(jax.random.normal(key, (2, D), jnp.float32), -3.0, 3.0)
    return (1.0 + 0.15 * normal_draw).astype(jnp.float32)


def with_spikes(values, key, source, target, parts, factor):
    owner, partner = [(jnp.arange(values.shape[axis_at]) // (values.shape[axis_at] // parts)).reshape([-1 if axis == axis_at else 1 for axis in range(values.ndim)]) for axis_at in (source, target)]
    chosen = jax.random.permutation(key, parts)[partner]
    strong = (owner == chosen) | (owner == (partner + parts // 2) % parts)
    return jnp.where(strong, factor * values, values)


def block_levels(own_key, shape, cuts, low, high):
    level = 1.0
    for dim, blocks in cuts:
        steps = jax.random.uniform(jax.random.fold_in(jax.random.fold_in(own_key, 6), dim), (blocks,), jnp.float32, low / len(cuts), high / len(cuts))
        level = level * jnp.repeat(jnp.exp(steps), shape[dim] // blocks).reshape((-1,) + (1,) * (len(shape) - 1 - dim))
    return level


def scatter_about(key, dims, scale, bound, cuts=(), dtype=jnp.bfloat16):
    drawn = jax.random.normal(key, dims, jnp.float32) * scale
    if len(cuts) > 0:
        drawn = block_levels(key, dims, cuts, -0.22, 0.18) * drawn
    return jnp.clip(drawn, min=-bound, max=bound).astype(dtype)


def heavy_noise(key, dims, scale, bound, cuts, heavy, dtype=jnp.bfloat16):
    values = scale * jax.random.normal(key, dims, jnp.float32)
    if cuts:
        values = values * block_levels(key, dims, cuts, -0.22, 0.18)
    return jnp.clip(with_spikes(values, jax.random.fold_in(key, 3), *heavy), -bound, bound).astype(dtype)


def setup_inputs(seed: int = 0) -> dict:
    streams_of = jax.random.split(jax.random.key(seed), 19)
    return {
        "inputs": heavy_noise(streams_of[0], (IMAGES, SEQ, D), 1.0, 6.0, ((0, 16),), (0, 2, 16, 2.0), jnp.float32),
        "out_grad": heavy_noise(streams_of[1], (IMAGES, SEQ, D), 1.0, 6.0, ((0, 16),), (0, 2, 16, 2.0), jnp.float32),
        "counts": draw_counts(jax.random.fold_in(streams_of[18], 71), 0),
        "qkv_weight": scatter_about(streams_of[3], (3, D, D), D ** -0.5, 0.3125, ((1, 16), (2, 2)), jnp.float32),
        "out_weight": scatter_about(streams_of[4], (D, D), (D * 4 // SEQ) ** -0.5, 3.0, ((0, 2), (1, 16)), jnp.float32),
        "up_weight": scatter_about(streams_of[5], (D, FF), D ** -0.5, 0.3125, ((0, 16), (1, 2)), jnp.float32),
        "down_weight": scatter_about(streams_of[6], (FF, D), FF ** -0.5, 0.15625, ((0, 2), (1, 16)), jnp.float32),
        "norm_vectors": draw_norm_vectors(jax.random.fold_in(streams_of[18], 71), 0),
        "qkv_first": scatter_about(streams_of[8], (3, D, D), (0.5 * TOKENS ** 0.5), 640.0, ((1, 16), (2, 2)), jnp.float32),
        "out_first": scatter_about(streams_of[9], (D, D), (0.1 * TOKENS ** 0.5), 128.0, ((0, 2), (1, 16)), jnp.float32),
        "up_first": scatter_about(streams_of[10], (D, FF), (0.3 * TOKENS ** 0.5), 384.0, ((0, 16), (1, 2)), jnp.float32),
        "down_first": scatter_about(streams_of[11], (FF, D), (0.5 * TOKENS ** 0.5), 640.0, ((0, 2), (1, 16)), jnp.float32),
        "norm_first": scatter_about(streams_of[12], (2, D), (0.5 * TOKENS ** 0.5), 640.0, ((1, 16),), jnp.float32),
        "qkv_second": jnp.clip(jnp.exp(math.log(49152.0) - 1.3862944 * jax.random.uniform(streams_of[13], (3, D, D), jnp.float32) ** block_levels(streams_of[13], (3, D, D), ((1, 16), (2, 2)), -0.2, 0.2)), 12288.0, 49152.0),
        "out_second": jnp.clip(jnp.exp(math.log(1966.08) - 1.3862944 * jax.random.uniform(streams_of[14], (D, D), jnp.float32) ** block_levels(streams_of[14], (D, D), ((0, 2), (1, 16)), -0.2, 0.2)), 491.52, 1966.08),
        "up_second": jnp.clip(jnp.exp(math.log(17694.72) - 1.3862944 * jax.random.uniform(streams_of[15], (D, FF), jnp.float32) ** block_levels(streams_of[15], (D, FF), ((0, 16), (1, 2)), -0.2, 0.2)), 4423.68, 17694.72),
        "down_second": jnp.clip(jnp.exp(math.log(49152.0) - 1.3862944 * jax.random.uniform(streams_of[16], (FF, D), jnp.float32) ** block_levels(streams_of[16], (FF, D), ((0, 2), (1, 16)), -0.2, 0.2)), 12288.0, 49152.0),
        "norm_second": jnp.clip(jnp.exp(math.log(49152.0) - 1.3862944 * jax.random.uniform(streams_of[17], (2, D), jnp.float32) ** block_levels(streams_of[17], (2, D), ((1, 16),), -0.2, 0.2)), 12288.0, 49152.0),
    }


@jax.custom_vjp
def low(v):
    return lax.optimization_barrier(v.astype(jnp.bfloat16)).astype(jnp.float32)

@jax.custom_vjp
def low_back(v):
    return v

def low_keep(v):
    return (low(v), None)

def low_pass(kept, grad):
    return (grad,)

def back_keep(v):
    return (v, None)

def back_low(kept, grad):
    return (low(grad),)
low.defvjp(low_keep, low_pass)
low_back.defvjp(back_keep, back_low)
EPS_NORM = 1e-06
EPS_ADAM = 1e-08
BETA_FIRST = 0.5
BETA_SECOND = 0.5
DECAY_MATRIX = 0.01
RATE_QKV = 0.05
RATE_OUT = 0.2
RATE_UP = 0.05
RATE_DOWN = 0.03
RATE_NORM = 0.3
PRECISION_TOP = lax.Precision.HIGHEST

def layer_norm(activations, gain_row):
    center = lax.optimization_barrier(jnp.mean(activations, axis=-1, keepdims=True))
    shifted = activations - center
    spread = lax.optimization_barrier(jnp.mean(shifted * shifted, axis=-1, keepdims=True))
    return shifted * lax.rsqrt(spread + EPS_NORM) * gain_row

def one_image(params, image_pair):
    qkv_low, out_low, up_low, down_low, norm_low = params
    image_rows, live_count = image_pair
    normed = low(layer_norm(image_rows, norm_low[0]))
    projected = low_back(low(jnp.einsum('sd,cdf->csf', normed, qkv_low, precision=PRECISION_TOP)))
    heads_all = projected.reshape(3, SEQ, HEADS, HEAD_DIM).transpose(0, 2, 1, 3)
    query_rows, key_rows, value_rows = (heads_all[0], heads_all[1], heads_all[2])
    raw_scores = low_back(jnp.einsum('hqe,hke->hqk', query_rows, key_rows, precision=PRECISION_TOP) * HEAD_DIM ** (-0.5))
    live_keys = jnp.arange(SEQ).astype(jnp.int32) < PATCHES + live_count
    masked = jnp.where(live_keys[None, None, :], raw_scores, -1e+30)
    row_top = lax.optimization_barrier(jnp.max(masked, axis=-1, keepdims=True))
    exponent = jnp.exp(masked - row_top)
    probs_full = exponent / lax.optimization_barrier(jnp.sum(exponent, axis=-1, keepdims=True))
    blended_heads = low_back(low(jnp.einsum('hqk,hke->hqe', low(probs_full), value_rows, precision=PRECISION_TOP)))
    merged = blended_heads.transpose(1, 0, 2).reshape(SEQ, D)
    middle = image_rows + low_back(jnp.dot(merged, out_low, precision=PRECISION_TOP))
    normed_two = low(layer_norm(middle, norm_low[1]))
    hidden = low_back(jnp.dot(normed_two, up_low, precision=PRECISION_TOP))
    active = low(jax.nn.gelu(hidden, approximate=False))
    return middle + low_back(jnp.dot(active, down_low, precision=PRECISION_TOP))

def forward(image_batch, qkv_weight, out_weight, up_weight, down_weight, norm_vectors, counts):
    params = (low(qkv_weight), low(out_weight), low(up_weight), low(down_weight), low(norm_vectors))
    one_step = jax.checkpoint(lambda image_pair: one_image(params, image_pair))
    return lax.map(one_step, (image_batch, counts))

def adamw_update(weight, gradient, first_moment, second_moment, step_rate, decay_rate):
    first_next = BETA_FIRST * first_moment + (1.0 - BETA_FIRST) * gradient
    second_next = BETA_SECOND * second_moment + (1.0 - BETA_SECOND) * gradient * gradient
    first_fixed = first_next / (1.0 - BETA_FIRST ** STEP)
    second_fixed = second_next / (1.0 - BETA_SECOND ** STEP)
    weight_next = weight - step_rate * (first_fixed / (jnp.sqrt(second_fixed) + EPS_ADAM) + decay_rate * weight)
    return (weight_next, first_next, second_next)

def reference(inputs, out_grad, counts, qkv_weight, out_weight, up_weight, down_weight, norm_vectors, qkv_first, out_first, up_first, down_first, norm_first, qkv_second, out_second, up_second, down_second, norm_second):

    def apply_block(image_batch, qkv_part, out_part, up_part, down_part, norm_part):
        return forward(image_batch, qkv_part, out_part, up_part, down_part, norm_part, counts)
    block_out, pullback = jax.vjp(apply_block, inputs, qkv_weight, out_weight, up_weight, down_weight, norm_vectors)
    input_grad, qkv_grad, out_grad_w, up_grad, down_grad, norm_grad = pullback(out_grad)
    qkv_new, qkv_first_new, qkv_second_new = adamw_update(qkv_weight, qkv_grad, qkv_first, qkv_second, RATE_QKV, DECAY_MATRIX)
    out_new, out_first_new, out_second_new = adamw_update(out_weight, out_grad_w, out_first, out_second, RATE_OUT, DECAY_MATRIX)
    up_new, up_first_new, up_second_new = adamw_update(up_weight, up_grad, up_first, up_second, RATE_UP, DECAY_MATRIX)
    down_new, down_first_new, down_second_new = adamw_update(down_weight, down_grad, down_first, down_second, RATE_DOWN, DECAY_MATRIX)
    norm_vectors_updated, norm_first_new, norm_second_new = adamw_update(norm_vectors, norm_grad, norm_first, norm_second, RATE_NORM, 0.0)
    return (block_out, input_grad, qkv_new, out_new, up_new, down_new, norm_vectors_updated, qkv_first_new, out_first_new, up_first_new, down_first_new, norm_first_new, qkv_second_new, out_second_new, up_second_new, down_second_new, norm_second_new, qkv_grad, out_grad_w, up_grad, down_grad, norm_grad)
```

```python
import functools
import types

import jax
import jax.numpy as jnp
from jax import lax
from jax.experimental import pallas as pl
from jax.experimental.pallas import tpu as pltpu
from jax.sharding import PartitionSpec as P

MESH = pl.DeviceIdType.MESH
bf = jnp.bfloat16
f32 = jnp.float32
S = 384
D = 384
NN=(((1,),(0,)),((),())); NT=(((1,),(1,)),((),())); TN=(((0,),(0,)),((),()))
def dot(a,b,dn=NN): return lax.dot_general(a,b,dn,preferred_element_type=f32)

def ln_stats(x):
    c = x - jnp.mean(x,axis=-1,keepdims=True)
    r = lax.rsqrt(jnp.mean(c*c,axis=-1,keepdims=True)+1e-6)
    return c*r, r

def gelu_parts(u):
    z = jnp.abs(u)*0.7071067811865476
    t = 1.0/(1.0+0.3275911*z)
    poly = t*(0.127414796 + t*(-0.142248368 + t*(0.7107068705 + t*(-0.7265760135 + t*0.5307027145))))
    E = jnp.exp(u*u*-0.5)
    h = poly*E
    phi = jnp.where(u>=0, 1.0-h, h)
    return phi, E*0.3989422804014327

def stack2(t, lo):
    z=jnp.zeros_like(t)
    return jnp.concatenate([jnp.where(lo,t,z),jnp.where(lo,z,t)],axis=0)

def unstackT(t):
    return jnp.concatenate([t[:64,:S],t[64:,S:]],axis=0).T

def a1(img, R, count):
    xh,_ = ln_stats(R.x[img])
    h1=(xh*R.g1).astype(bf)
    R.h1[img]=h1
    for b in range(3):
        for m in range(3):
            c=m*384+128*b
            R.qkv[img,:,c:c+128]=dot(h1,R.wqkv[:,c:c+128]).astype(bf)
    lo=lax.broadcasted_iota(jnp.int32,(S,128),1)<64
    for b in range(3):
        q=R.qkv[img,:,128*b:128*b+128]*jnp.asarray(0.125,bf)
        k=R.qkv[img,:,384+128*b:512+128*b]
        v=R.qkv[img,:,768+128*b:896+128*b]
        q2=stack2(q,lo)
        s=dot(k,q2,NT)
        key=lax.broadcasted_iota(jnp.int32,(128,2*S),0)
        s=jnp.concatenate([s[:256],jnp.where(key<count,s[256:],-1e30)],axis=0)
        mx=jnp.max(s,axis=0,keepdims=True)
        e=jnp.exp(s-mx)
        p=e*(1.0/jnp.sum(e,axis=0,keepdims=True))
        R.p[img,b]=p
        oT=dot(v,p.astype(bf),TN)
        R.o[img,:,128*b:128*b+128]=unstackT(oT).astype(bf)

CH=512
def a2(img, R):
    o=R.o[img]; x=R.x[img]; g=R.g[img]
    y1=x+dot(o,R.wo[...],NT)
    xh2,r2=ln_stats(y1)
    h2=(xh2*R.g2).astype(bf)
    dl=g.astype(bf)
    bo=y1; dh2=jnp.zeros((S,D),f32)
    for c0 in range(0,1536,CH):
        c=slice(c0,c0+CH)
        u=dot(h2,R.wu[:,c])
        da=dot(dl,R.wd[:,c])
        phi,ph=gelu_parts(u)
        a=(u*phi).astype(bf)
        du=(da*(phi+u*ph)).astype(bf)
        bo=bo+dot(a,R.wd[:,c],NT)
        dh2=dh2+dot(du,R.wu[:,c],NT)
        R.Gu[:,c]=R.Gu[:,c]+dot(h2,du,TN)
        R.Gd[:,c]=R.Gd[:,c]+dot(dl,a,TN)
    R.bo[img]=bo.astype(R.bo.dtype)
    e=dh2*R.g2
    m1=jnp.mean(e,axis=-1,keepdims=True)
    m2=jnp.mean(e*xh2,axis=-1,keepdims=True)
    dy=g+r2*(e-m1-xh2*m2)
    R.dy[img]=dy
    R.gn[1:2,:]=R.gn[1:2,:]+jnp.sum(dh2*xh2,axis=0,keepdims=True)
    R.Go[...]=R.Go[...]+dot(dy.astype(bf),o,TN)

def cc(img, R):
    dy=R.dy[img]
    dm=dy.astype(bf)
    h1=R.h1[img]
    lo=lax.broadcasted_iota(jnp.int32,(S,128),1)<64
    dh1=jnp.zeros((S,D),f32)
    for b in range(3):
        sl=slice(128*b,128*b+128)
        do=dot(dm,R.wo[:,sl]).astype(bf)
        do2=stack2(do,lo)
        q2=stack2(R.qkv[img,:,sl]*jnp.asarray(0.125,bf),lo)
        k=R.qkv[img,:,384+128*b:512+128*b]
        v=R.qkv[img,:,768+128*b:896+128*b]
        p=R.p[img,b]
        dv=dot(p.astype(bf),do2).astype(bf)
        dp=dot(v,do2,NT)
        inner=jnp.sum(p*dp,axis=0,keepdims=True)
        ds=(p*(dp-inner)).astype(bf)
        dk=dot(ds,q2).astype(bf)
        dq=(unstackT(dot(k,ds,TN))*0.125).astype(bf)
        R.dqkv[:,sl]=dq; R.dqkv[:,384+128*b:512+128*b]=dk; R.dqkv[:,768+128*b:896+128*b]=dv
    dqkv=R.dqkv[...]
    R.Gqkv[...]=R.Gqkv[...]+dot(h1,dqkv,TN)
    dh1=dot(dqkv,R.wqkv[...],NT)
    xh1,r1=ln_stats(R.x[img])
    e=dh1*R.g1
    m1=jnp.mean(e,axis=-1,keepdims=True)
    m2=jnp.mean(e*xh1,axis=-1,keepdims=True)
    ig=dy+r1*(e-m1-xh1*m2)
    R.ig[img]=ig.astype(R.ig.dtype)
    R.gn[0:1,:]=R.gn[0:1,:]+jnp.sum(dh1*xh1,axis=0,keepdims=True)


STEP = 5
EPS_ADAM = 1e-08
BETA_FIRST = 0.5
BETA_SECOND = 0.5
DECAY_MATRIX = 0.01
RATE_QKV = 0.05
RATE_OUT = 0.2
RATE_UP = 0.05
RATE_DOWN = 0.03
RATE_NORM = 0.3


class Plan:
    def __init__(self, dp, mp, rows, images):
        assert mp == 2 and dp & (dp - 1) == 0
        self.dp, self.mp, self.rows = dp, mp, rows
        self.bits = dp.bit_length() - 1
        self.stages = self.bits + 1
        self.slots = dp * mp
        self.folded = -(-2 * rows // 16) * 16
        self.images = images
        self.here = images // mp
        high = [("dp", b) for b in range(self.bits - 1, 1, -1)]
        x, y, core = ("mp", 0), ("dp", 1), ("dp", 0)
        self.gather = [
            (0, 2, high + [x, y, core]),
            (2, 1, high + [y, x, core]),
            (3, 2, high + [x, y, core]),
            (5, 4, high + [y, x, core]),
        ]
        self.scatter = [
            (0, 2, high + [x, y, core]),
            (2, 1, high + [y, x, core]),
            (3, 2, high + [x, y, core]),
            (5, 4, high + [y, x, core]),
        ]


def slot_of(order, i, j):
    total = 0
    for t, (axis, b) in enumerate(order):
        bit = j if axis == "mp" else (i // 2**b) % 2
        total = total + bit * 2**t
    return total


class Place:
    def __init__(self):
        self.i = lax.axis_index("dp")
        self.j = lax.axis_index("mp")

    def bit(self, axis_bit):
        axis, b = axis_bit
        return self.j if axis == "mp" else lax.rem(self.i // 2**b, 2)

    def partner(self, axis_bit):
        axis, b = axis_bit
        if axis == "mp":
            return {"mp": 1 - self.j}
        return {"dp": self.i + 2**b - 2 ** (b + 1) * self.bit(axis_bit)}

    def slot(self, order):
        total = 0
        for t, axis_bit in enumerate(order):
            total = total + self.bit(axis_bit) * 2**t
        return total


def remote(src, dst, send, recv, where):
    return pltpu.make_async_remote_copy(
        src_ref=src, dst_ref=dst, send_sem=send, recv_sem=recv, device_id=where, device_id_type=MESH
    )


class Gather:
    def __init__(self, place, order, buf, send, recv):
        self.place, self.order, self.buf = place, order, buf
        self.send, self.recv = send, recv
        self.slot = place.slot(order)

    def copy(self, t):
        size = 2**t
        start = self.slot - lax.rem(self.slot, size)
        part = self.buf.at[pl.ds(start, size)]
        return remote(
            part, part, self.send.at[t], self.recv.at[t], self.place.partner(self.order[t])
        )

    def start(self, t):
        self.copy(t).start()

    def wait(self, t):
        self.copy(t).wait_recv()

    def finish(self):
        for t in range(len(self.order)):
            self.copy(t).wait_send()


class Scatter:
    def __init__(self, place, order, total, out, came, send, recv):
        self.place, self.order, self.total = place, order, total
        self.out, self.came, self.send, self.recv = out, came, send, recv
        self.top = len(order) - 1
        self.own = place.slot(order[:-1])

    def copy(self, t):
        size = 2**t
        here = pl.ds(size, size)
        return remote(
            self.out.at[here],
            self.came.at[here],
            self.send.at[t],
            self.recv.at[t],
            self.place.partner(self.order[t]),
        )

    def kept(self, t):
        return self.own - lax.rem(self.own, 2**t)

    def start(self, t):
        if t < self.top:
            size = 2**t
            base = self.own - lax.rem(self.own, 2 * size)
            away = base + (1 - self.place.bit(self.order[t])) * size
            self.out[pl.ds(size, size)] = self.total[pl.ds(away, size)].astype(bf)
        self.copy(t).start()

    def add(self, t):
        size = 2**t
        self.copy(t).wait_recv()
        keep = 0 if t == self.top else self.kept(t)
        self.total[pl.ds(keep, size)] = self.total[pl.ds(keep, size)] + self.came[
            pl.ds(size, size)
        ].astype(f32)

    def finish(self):
        for t in range(self.top + 1):
            self.copy(t).wait_send()


def low_half(rows):
    return lax.broadcasted_iota(jnp.int32, (rows, 128), 1) < 64


def unpack(plan, groups, bufs, R, which):
    rows = plan.rows
    step = 16
    while step % rows and (step // 16) < 64:
        step += 16
    per = max(step // rows, 1)
    if (per * rows) % 16:
        raise ValueError("rows")
    first, last = (0, 3) if which == "A" else (3, 9)
    for m in range(plan.dp // per):
        tops, bottoms = [[], []], [[], []]
        for j in range(2):
            for f in range(first, last):
                g = next(n for n, e in enumerate(groups) if e[0] <= f < e[0] + e[1])
                lane = 128 * (f - groups[g][0])
                parts = [
                    bufs[g][slot_of(groups[g][2], m * per + n, j), :, lane : lane + 128].astype(f32)
                    for n in range(per)
                ]
                tops[j].append(jnp.concatenate([q[:rows] for q in parts], axis=0))
                bottoms[j].append(jnp.concatenate([q[rows : 2 * rows] for q in parts], axis=0))
        c0, c1 = tops[0] + bottoms[0], tops[1] + bottoms[1]
        size = per * rows
        lo = low_half(size)
        at = slice(m * size, (m + 1) * size)

        def put(ref, block, value):
            ref[at, 128 * block : 128 * block + 128] = value.astype(bf)

        if which == "A":
            for n in range(3):
                put(R.wqkv, 3 * n, c0[n])
                put(R.wqkv, 3 * n + 1, jnp.where(lo, c0[3 + n], c1[3 + n]))
                put(R.wqkv, 3 * n + 2, c1[n])
            put(R.wu, 10, jnp.where(lo, c1[3], c0[3]))
            put(R.wu, 11, jnp.where(lo, c1[4], c0[4]))
            put(R.wd, 10, jnp.where(lo, c1[5], c0[5]))
        else:
            put(R.wo, 0, c0[0])
            put(R.wo, 1, jnp.where(lo, c0[1], c1[1]))
            put(R.wo, 2, c1[0])
            put(R.wd, 11, jnp.where(lo, c1[1], c0[1]))
            for n in range(5):
                put(R.wu, n, c0[2 + n])
                put(R.wu, 5 + n, c1[2 + n])
                put(R.wd, n, c0[7 + n])
                put(R.wd, 5 + n, c1[7 + n])


def pack(plan, groups, scatters, R, core, which):
    rows = plan.rows
    lo = low_half(2 * rows)
    first, last = (0, 3) if which == "A" else (3, 9)
    for r in range(plan.dp // 2):
        at = slice(2 * r * rows, 2 * (r + 1) * rows)

        def get(ref, block):
            return ref[at, 128 * block : 128 * block + 128]

        def piece(j, n):
            if which == "A":
                if n < 3:
                    return get(R.Gqkv, 3 * n + 2 * j)
                own = get(R.Gqkv, 3 * (n - 3) + 1)
                fill = get(R.Gu, 7 + n) if n < 5 else get(R.Gd, 10)
            elif n == 0:
                return get(R.Go, 2 * j)
            elif n == 1:
                own, fill = get(R.Go, 1), get(R.Gd, 11)
            elif n < 7:
                return get(R.Gu, n - 2 + 5 * j)
            else:
                return get(R.Gd, n - 7 + 5 * j)
            return jnp.where(lo, own, fill) if j == 0 else jnp.where(lo, fill, own)

        for j in range(2):
            for f in range(first, last):
                g = next(n for n, e in enumerate(groups) if e[0] <= f < e[0] + e[1])
                lane = 128 * (f - groups[g][0])
                n = f - first
                top, bottom = piece(j, n), piece(j, n + last - first)
                even = jnp.concatenate([top[:rows], bottom[:rows]], axis=0)
                odd = jnp.concatenate([top[rows:], bottom[rows:]], axis=0)
                if plan.folded > 2 * rows:
                    none = jnp.zeros((plan.folded - 2 * rows, 128), f32)
                    even = jnp.concatenate([even, none], axis=0)
                    odd = jnp.concatenate([odd, none], axis=0)
                slot = slot_of(groups[g][2][:-1], 2 * r, j)
                half = plan.slots // 2
                scatters[g].out[half + slot, :, lane : lane + 128] = jnp.where(
                    core == 0, odd, even
                ).astype(bf)
                scatters[g].total[slot, :, lane : lane + 128] = jnp.where(core == 0, even, odd)


def layer_kernel(plan, *refs):
    it = iter(refs)
    take = lambda n: [next(it) for _ in range(n)]
    counts, inputs, out_grad, packed, gpos = take(5)
    bo_out, ig_out, grads_out, gn_out = take(4)
    x, g, h1, qkv, p, o, dy, dqkv = take(8)
    wqkv, wo, wu, wd, Gqkv, Go, Gu, Gd, gn = take(9)
    bo, ig = take(2)
    ng = len(plan.gather)
    gbufs = take(ng)
    g_send, g_recv = take(2)
    ns = len(plan.scatter)
    totals, outs, cames = take(ns), take(ns), take(ns)
    s_send, s_recv = take(2)
    gains, gains_in, gains_send, gains_recv = take(4)
    sums, sums_in, sums_send, sums_recv = take(4)
    load_sem, store_sem, x_send, x_recv = take(4)

    place = Place()
    j = place.j
    every = [("dp", b) for b in range(plan.bits)] + [("mp", 0)]
    here = plan.here

    loads = []
    for n in range(here):
        for k, (src, dst) in enumerate(((inputs, x), (out_grad, g))):
            loads.append(
                pltpu.make_async_copy(src.at[j * here + n], dst.at[n], load_sem.at[k, n])
            )
    for c in loads:
        c.start()

    barrier = pltpu.get_barrier_semaphore()
    for axis_bit in every:
        pl.semaphore_signal(
            barrier, inc=1, device_id=place.partner(axis_bit), device_id_type=MESH
        )

    gathers = [
        Gather(place, order, gbufs[n], g_send.at[n], g_recv.at[n])
        for n, (_, _, order) in enumerate(plan.gather)
    ]
    for n, (f, size, _) in enumerate(plan.gather):
        gbufs[n][gathers[n].slot] = packed[:, 128 * f : 128 * (f + size)]
    gains[0] = gpos[...]
    scatters = [
        Scatter(place, order, totals[n], outs[n], cames[n], s_send.at[n], s_recv.at[n])
        for n, (_, _, order) in enumerate(plan.scatter)
    ]
    first = [n for n in range(ng) if plan.gather[n][0] < 3]
    second = [n for n in range(ng) if plan.gather[n][0] >= 3]
    early = [n for n in range(ns) if plan.scatter[n][0] >= 3]
    late = [n for n in range(ns) if plan.scatter[n][0] < 3]
    top = plan.stages - 1

    gain_order = [("dp", b) for b in range(plan.bits - 1, -1, -1)]

    def gain_copy(t):
        return remote(
            gains.at[t],
            gains_in.at[t],
            gains_send.at[t],
            gains_recv.at[t],
            place.partner(gain_order[t]),
        )

    sum_order = gain_order + [("mp", 0)]

    def sum_copy(t):
        return remote(
            sums.at[t], sums_in.at[t], sums_send.at[t], sums_recv.at[t], place.partner(sum_order[t])
        )

    pl.semaphore_wait(barrier, len(every))

    for t in range(plan.stages):
        for n in first:
            if t:
                gathers[n].wait(t - 1)
            gathers[n].start(t)
        if t < plan.bits:
            if t:
                gain_copy(t - 1).wait_recv()
                gains[t] = gains[t - 1] + gains_in[t - 1]
            gain_copy(t).start()
        if t < top - 1:
            for n in second:
                if t:
                    gathers[n].wait(t - 1)
                gathers[n].start(t)
        if t == 0:
            for ref in (Gqkv, Go, Gu, Gd, gn):
                ref[...] = jnp.zeros_like(ref)
    gain_copy(plan.bits - 1).wait_recv()
    gains[plan.bits] = gains[plan.bits - 1] + gains_in[plan.bits - 1]
    for n in first:
        gathers[n].wait(top)
    R = types.SimpleNamespace(
        x=x, g=g, h1=h1, qkv=qkv, p=p, o=o, dy=dy, dqkv=dqkv, wqkv=wqkv, wo=wo, wu=wu, wd=wd,
        Gqkv=Gqkv, Go=Go, Gu=Gu, Gd=Gd, gn=gn, bo=bo, ig=ig,
    )
    unpack(plan, plan.gather, gbufs, R, "A")
    R.g1 = gains[plan.bits, 0:1, :]
    R.g2 = gains[plan.bits, 1:2, :]

    for n in second:
        gathers[n].wait(top - 2)
        gathers[n].start(top - 1)
    for c in loads:
        c.wait()

    def attend(n, carry):
        a1(n, R, counts[j * here + n])

        @pl.when(n == (here - 1) // 2)
        def _():
            for k in second:
                gathers[k].wait(top - 1)
                gathers[k].start(top)

        return carry

    lax.fori_loop(0, here, attend, 0)
    for n in second:
        gathers[n].wait(top)
    unpack(plan, plan.gather, gbufs, R, "B")

    def swap(n, k):
        ref, out = ((bo, bo_out), (ig, ig_out))[k]
        return (
            pltpu.make_async_copy(ref.at[n], out.at[j * here + n], store_sem.at[k, n]),
            remote(
                ref.at[n], out.at[j * here + n], x_send.at[k, n], x_recv.at[k, n], {"mp": 1 - j}
            ),
        )

    def feed(n, carry):
        a2(n, R)
        for c in swap(n, 0):
            c.start()
        return carry

    lax.fori_loop(0, here, feed, 0)

    core = place.bit(("dp", 0))
    pack(plan, plan.scatter, scatters, R, core, "B")
    for n in early:
        scatters[n].start(top)

    marks = [top - 1 - ((top + 1) * n) // here for n in range(here)]

    def back(n, carry):
        cc(n, R)
        for c in swap(n, 1):
            c.start()
        t_done = top
        for image in range(here - 1):
            stages = list(range(t_done, max(t_done - 2, 0) if image else t_done - 1, -1))[:2]
            stages = stages[:1] if image < here - 2 else stages

            @pl.when(n == image)
            def _(stages=stages):
                for t in stages:
                    for k in early:
                        scatters[k].add(t)
                        if t:
                            scatters[k].start(t - 1)

            t_done = stages[-1] - 1 if stages else t_done
        back.t_done = t_done
        return carry

    lax.fori_loop(0, here, back, 0)

    pack(plan, plan.scatter, scatters, R, core, "A")
    sums[0] = gn[...]
    for n in late:
        scatters[n].start(top)
    sum_copy(0).start()
    t_early = back.t_done
    for step in range(top + 1):
        t = top - step
        for n in late:
            scatters[n].add(t)
            if t:
                scatters[n].start(t - 1)
        sum_copy(step).wait_recv()
        sums[step + 1] = sums[step] + sums_in[step]
        if step < top:
            sum_copy(step + 1).start()
        if t_early >= 0:
            for n in early:
                scatters[n].add(t_early)
                if t_early:
                    scatters[n].start(t_early - 1)
            t_early -= 1
    for n, (f, size, _) in enumerate(plan.scatter):
        grads_out[:, 128 * f : 128 * (f + size)] = totals[n][scatters[n].own]
    gn_out[...] = sums[plan.stages]

    for c in gathers + scatters:
        c.finish()
    for t in range(plan.bits):
        gain_copy(t).wait_send()
    for t in range(plan.stages):
        sum_copy(t).wait_send()
    for n in range(here):
        for k in range(2):
            own, away = swap(n, k)
            own.wait()
            away.wait()


def run_layer(plan, counts, inputs, out_grad, packed, gpos):
    here, slots, folded = plan.here, plan.slots, plan.folded
    vmem = pl.BlockSpec(memory_space=pltpu.VMEM)
    hbm = pl.BlockSpec(memory_space=pl.ANY)
    dma = pltpu.SemaphoreType.DMA
    out = jax.ShapeDtypeStruct
    ng, ns = len(plan.gather), len(plan.scatter)
    lanes_g = [128 * e[1] for e in plan.gather]
    lanes_s = [128 * e[1] for e in plan.scatter]
    scratch = [
        pltpu.VMEM((here, S, D), f32),
        pltpu.VMEM((here, S, D), f32),
        pltpu.VMEM((here, S, D), bf),
        pltpu.VMEM((here, S, 3 * D), bf),
        pltpu.VMEM((here, 3, S, 2 * S), f32),
        pltpu.VMEM((here, S, D), bf),
        pltpu.VMEM((here, S, D), f32),
        pltpu.VMEM((S, 3 * D), bf),
        pltpu.VMEM((D, 3 * D), bf),
        pltpu.VMEM((D, D), bf),
        pltpu.VMEM((D, 4 * D), bf),
        pltpu.VMEM((D, 4 * D), bf),
        pltpu.VMEM((D, 3 * D), f32),
        pltpu.VMEM((D, D), f32),
        pltpu.VMEM((D, 4 * D), f32),
        pltpu.VMEM((D, 4 * D), f32),
        pltpu.VMEM((8, D), f32),
        pltpu.VMEM((here, S, D), bf),
        pltpu.VMEM((here, S, D), bf),
    ]
    scratch += [pltpu.VMEM((slots, folded, n), bf) for n in lanes_g]
    scratch += [dma((ng, plan.stages)), dma((ng, plan.stages))]
    scratch += [pltpu.VMEM((slots // 2, folded, n), f32) for n in lanes_s]
    scratch += [pltpu.VMEM((slots, folded, n), bf) for n in lanes_s]
    scratch += [pltpu.VMEM((slots, folded, n), bf) for n in lanes_s]
    scratch += [dma((ns, plan.stages)), dma((ns, plan.stages))]
    scratch += [
        pltpu.VMEM((plan.bits + 1, 8, D), f32),
        pltpu.VMEM((plan.bits, 8, D), f32),
        dma((plan.bits,)),
        dma((plan.bits,)),
        pltpu.VMEM((plan.stages + 1, 8, D), f32),
        pltpu.VMEM((plan.stages, 8, D), f32),
        dma((plan.stages,)),
        dma((plan.stages,)),
        dma((2, here)),
        dma((2, here)),
        dma((2, here)),
        dma((2, here)),
    ]
    return pl.pallas_call(
        functools.partial(layer_kernel, plan),
        out_shape=[
            out(inputs.shape, bf),
            out(inputs.shape, bf),
            out((folded, 9 * 128), f32),
            out((8, D), f32),
        ],
        in_specs=[pl.BlockSpec(memory_space=pltpu.SMEM), hbm, hbm, vmem, vmem],
        out_specs=[hbm, hbm, vmem, vmem],
        scratch_shapes=scratch,
        compiler_params=pltpu.CompilerParams(
            collective_id=0, has_side_effects=True, vmem_limit_bytes=63 << 20
        ),
        name="layer",
    )(counts, inputs, out_grad, packed, gpos)


def fold(a, folded):
    half = a.shape[1] // 2
    out = jnp.concatenate([a[:, :half], a[:, half:]], axis=0)
    return jnp.pad(out, ((0, folded - out.shape[0]), (0, 0)))


def adamw_update(weight, gradient, first_moment, second_moment, step_rate, decay_rate):
    first_next = BETA_FIRST * first_moment + (1.0 - BETA_FIRST) * gradient
    second_next = BETA_SECOND * second_moment + (1.0 - BETA_SECOND) * gradient * gradient
    first_fixed = first_next / (1.0 - BETA_FIRST**STEP)
    second_fixed = second_next / (1.0 - BETA_SECOND**STEP)
    weight_next = weight - step_rate * (
        first_fixed / (jnp.sqrt(second_fixed) + EPS_ADAM) + decay_rate * weight
    )
    return (weight_next, first_next, second_next)


def shards(
    dp, mp, inputs, out_grad, counts,
    qkv_weight, out_weight, up_weight, down_weight, norm_vectors,
    qkv_first, out_first, up_first, down_first, norm_first,
    qkv_second, out_second, up_second, down_second, norm_second,
):
    rows = up_weight.shape[0]
    plan = Plan(dp, mp, rows, inputs.shape[0])
    i, j = lax.axis_index("dp"), lax.axis_index("mp")
    oT, dT, u = out_weight.T, down_weight.T, up_weight
    q, k, v = qkv_weight[0], qkv_weight[1], qkv_weight[2]

    def mix(own, fill):
        return jnp.where(
            j == 0,
            jnp.concatenate([own, fill], axis=1),
            jnp.concatenate([fill, own], axis=1),
        )

    part_a = jnp.concatenate(
        [
            q[:, :128], k[:, :128], v[:, :128],
            mix(q[:, 128:], u[:, 640:704]),
            mix(k[:, 128:], u[:, 704:]),
            mix(v[:, 128:], dT[:, 640:704]),
        ],
        axis=1,
    )
    part_b = jnp.concatenate(
        [oT[:, :128], mix(oT[:, 128:], dT[:, 704:]), u[:, :640], dT[:, :640]], axis=1
    )
    packed = jnp.concatenate(
        [fold(part_a, plan.folded), fold(part_b, plan.folded)], axis=1
    ).astype(bf)
    rounded = lax.reduce_precision(norm_vectors, 8, 7)
    gpos = lax.dynamic_update_slice(jnp.zeros((8, D), f32), rounded, (0, i * rows))

    bo, ig, grads, sums = run_layer(plan, counts, inputs, out_grad, packed, gpos)

    ga = jnp.concatenate([grads[:rows, :384], grads[rows : 2 * rows, :384]], axis=1)
    gb = jnp.concatenate([grads[:rows, 384:], grads[rows : 2 * rows, 384:]], axis=1)

    def split(block):
        left, right = block[:, :64], block[:, 64:]
        return jnp.where(j == 0, left, right), jnp.where(j == 0, right, left)

    mixed = [split(ga[:, 384 + 128 * n : 512 + 128 * n]) for n in range(3)]
    mixed_o = split(gb[:, 128:256])
    qkv_grad = jnp.stack(
        [jnp.concatenate([ga[:, 128 * n : 128 * n + 128], mixed[n][0]], axis=1) for n in range(3)]
    )
    out_grad_w = jnp.concatenate([gb[:, :128], mixed_o[0]], axis=1).T
    up_grad = jnp.concatenate([gb[:, 256:896], mixed[0][1], mixed[1][1]], axis=1)
    down_grad = jnp.concatenate([gb[:, 896:], mixed[2][1], mixed_o[1]], axis=1).T
    norm_grad = lax.dynamic_slice(sums, (0, i * rows), (2, rows))

    new = [
        adamw_update(qkv_weight, qkv_grad, qkv_first, qkv_second, RATE_QKV, DECAY_MATRIX),
        adamw_update(out_weight, out_grad_w, out_first, out_second, RATE_OUT, DECAY_MATRIX),
        adamw_update(up_weight, up_grad, up_first, up_second, RATE_UP, DECAY_MATRIX),
        adamw_update(down_weight, down_grad, down_first, down_second, RATE_DOWN, DECAY_MATRIX),
        adamw_update(norm_vectors, norm_grad, norm_first, norm_second, RATE_NORM, 0.0),
    ]
    return (
        bo.astype(f32),
        ig.astype(f32),
        *[e[0] for e in new],
        *[e[1] for e in new],
        *[e[2] for e in new],
        qkv_grad, out_grad_w, up_grad, down_grad, norm_grad,
    )


def solution(mesh):
    stored = (
        P(None, "dp", "mp"),
        P("mp", "dp"),
        P("dp", "mp"),
        P("mp", "dp"),
        P(None, "dp"),
    )
    images = P("dp", None, None)
    return jax.shard_map(
        functools.partial(shards, mesh.shape["dp"], mesh.shape["mp"]),
        mesh=mesh,
        in_specs=(images, images, P("dp")) + stored * 3,
        out_specs=(images, images) + stored * 4,
        check_vma=False,
    )
```

```python
import functools
import types

import jax
import jax.numpy as jnp
from jax import lax
from jax.experimental import pallas as pl
from jax.experimental.pallas import tpu as pltpu
from jax.sharding import PartitionSpec as P

MESH = pl.DeviceIdType.MESH
bf = jnp.bfloat16
f32 = jnp.float32
S = 384
D = 384
NN=(((1,),(0,)),((),())); NT=(((1,),(1,)),((),())); TN=(((0,),(0,)),((),()))
def dot(a,b,dn=NN): return lax.dot_general(a,b,dn,preferred_element_type=f32)

def ln_stats(x):
    c = x - jnp.mean(x,axis=-1,keepdims=True)
    r = lax.rsqrt(jnp.mean(c*c,axis=-1,keepdims=True)+1e-6)
    return c*r, r

def gelu_parts(u):
    z = jnp.abs(u)*0.7071067811865476
    t = 1.0/(1.0+0.3275911*z)
    poly = t*(0.127414796 + t*(-0.142248368 + t*(0.7107068705 + t*(-0.7265760135 + t*0.5307027145))))
    E = jnp.exp(u*u*-0.5)
    h = poly*E
    phi = jnp.where(u>=0, 1.0-h, h)
    return phi, E*0.3989422804014327

def stack2(t, lo):
    z=jnp.zeros_like(t)
    return jnp.concatenate([jnp.where(lo,t,z),jnp.where(lo,z,t)],axis=0)

def unstackT(t):
    return jnp.concatenate([t[:64,:S],t[64:,S:]],axis=0).T

def a1(img, R, count):
    xh,_ = ln_stats(R.x[img])
    h1=(xh*R.g1).astype(bf)
    R.h1[img]=h1
    for b in range(3):
        for m in range(3):
            c=m*384+128*b
            R.qkv[img,:,c:c+128]=dot(h1,R.wqkv[:,c:c+128]).astype(bf)
    lo=lax.broadcasted_iota(jnp.int32,(S,128),1)<64
    for b in range(3):
        q=R.qkv[img,:,128*b:128*b+128]*jnp.asarray(0.125,bf)
        k=R.qkv[img,:,384+128*b:512+128*b]
        v=R.qkv[img,:,768+128*b:896+128*b]
        q2=stack2(q,lo)
        s=dot(k,q2,NT)
        key=lax.broadcasted_iota(jnp.int32,(128,2*S),0)
        s=jnp.concatenate([s[:256],jnp.where(key<count,s[256:],-1e30)],axis=0)
        mx=jnp.max(s,axis=0,keepdims=True)
        e=jnp.exp(s-mx)
        p=e*(1.0/jnp.sum(e,axis=0,keepdims=True))
        R.p[img,b]=p
        oT=dot(v,p.astype(bf),TN)
        R.o[img,:,128*b:128*b+128]=unstackT(oT).astype(bf)

CH=512
def a2(img, R):
    o=R.o[img]; x=R.x[img]; g=R.g[img]
    y1=x+dot(o,R.wo[...],NT)
    xh2,r2=ln_stats(y1)
    h2=(xh2*R.g2).astype(bf)
    dl=g.astype(bf)
    bo=y1; dh2=jnp.zeros((S,D),f32)
    for c0 in range(0,1536,CH):
        c=slice(c0,c0+CH)
        u=dot(h2,R.wu[:,c])
        da=dot(dl,R.wd[:,c])
        phi,ph=gelu_parts(u)
        a=(u*phi).astype(bf)
        du=(da*(phi+u*ph)).astype(bf)
        bo=bo+dot(a,R.wd[:,c],NT)
        dh2=dh2+dot(du,R.wu[:,c],NT)
        R.Gu[:,c]=R.Gu[:,c]+dot(h2,du,TN)
        R.Gd[:,c]=R.Gd[:,c]+dot(dl,a,TN)
    R.bo[img]=bo.astype(R.bo.dtype)
    e=dh2*R.g2
    m1=jnp.mean(e,axis=-1,keepdims=True)
    m2=jnp.mean(e*xh2,axis=-1,keepdims=True)
    dy=g+r2*(e-m1-xh2*m2)
    R.dy[img]=dy
    R.gn[1:2,:]=R.gn[1:2,:]+jnp.sum(dh2*xh2,axis=0,keepdims=True)
    R.Go[...]=R.Go[...]+dot(dy.astype(bf),o,TN)

def cc(img, R):
    dy=R.dy[img]
    dm=dy.astype(bf)
    h1=R.h1[img]
    lo=lax.broadcasted_iota(jnp.int32,(S,128),1)<64
    dh1=jnp.zeros((S,D),f32)
    for b in range(3):
        sl=slice(128*b,128*b+128)
        do=dot(dm,R.wo[:,sl]).astype(bf)
        do2=stack2(do,lo)
        q2=stack2(R.qkv[img,:,sl]*jnp.asarray(0.125,bf),lo)
        k=R.qkv[img,:,384+128*b:512+128*b]
        v=R.qkv[img,:,768+128*b:896+128*b]
        p=R.p[img,b]
        dv=dot(p.astype(bf),do2).astype(bf)
        dp=dot(v,do2,NT)
        inner=jnp.sum(p*dp,axis=0,keepdims=True)
        ds=(p*(dp-inner)).astype(bf)
        dk=dot(ds,q2).astype(bf)
        dq=(unstackT(dot(k,ds,TN))*0.125).astype(bf)
        R.dqkv[:,sl]=dq; R.dqkv[:,384+128*b:512+128*b]=dk; R.dqkv[:,768+128*b:896+128*b]=dv
    dqkv=R.dqkv[...]
    R.Gqkv[...]=R.Gqkv[...]+dot(h1,dqkv,TN)
    dh1=dot(dqkv,R.wqkv[...],NT)
    xh1,r1=ln_stats(R.x[img])
    e=dh1*R.g1
    m1=jnp.mean(e,axis=-1,keepdims=True)
    m2=jnp.mean(e*xh1,axis=-1,keepdims=True)
    ig=dy+r1*(e-m1-xh1*m2)
    R.ig[img]=ig.astype(R.ig.dtype)
    R.gn[0:1,:]=R.gn[0:1,:]+jnp.sum(dh1*xh1,axis=0,keepdims=True)


STEP = 5
EPS_ADAM = 1e-08
BETA_FIRST = 0.5
BETA_SECOND = 0.5
DECAY_MATRIX = 0.01
RATE_QKV = 0.05
RATE_OUT = 0.2
RATE_UP = 0.05
RATE_DOWN = 0.03
RATE_NORM = 0.3


class Plan:
    def __init__(self, dp, mp, rows, images):
        assert mp == 2 and dp >= 4 and dp & (dp - 1) == 0
        self.dp, self.mp, self.rows = dp, mp, rows
        self.bits = dp.bit_length() - 1
        self.slots = dp * mp
        self.folded = -(-2 * rows // 16) * 16
        self.images = images
        self.here = images // mp
        high = [("dp", b) for b in range(2, self.bits)]
        high = [high] if high else []
        x, y, core = [("mp", 0)], [("dp", 1)], [("dp", 0)]
        self.gather = [
            (0, 2, high + [x, y, core]),
            (2, 1, high + [y, x, core]),
            (3, 4, high + [y, x, core]),
            (7, 2, high + [x, y, core]),
        ]
        self.scatter = [
            (0, 2, [x] + high + [y, core]),
            (2, 1, [x, y] + high + [core]),
            (3, 4, [x] + high + [y, core]),
            (7, 2, [x, y] + high + [core]),
        ]
        self.gains = high + [y, core]
        self.sums = [core, y] + high + [x]

    def copies(self, stages):
        return sum(2 ** len(e) - 1 for e in stages)

    def partners(self):
        found = []
        for stages in [e[2] for e in self.gather + self.scatter] + [self.gains, self.sums]:
            for stage in stages:
                for d in range(1, 2 ** len(stage)):
                    flip = sorted(e for m, e in enumerate(stage) if (d >> m) & 1)
                    if flip not in found:
                        found.append(flip)
        return found


def slot_of(stages, i, j):
    total = 0
    for t, (axis, b) in enumerate(e for stage in stages for e in stage):
        bit = j if axis == "mp" else (i // 2**b) % 2
        total = total + bit * 2**t
    return total


class Place:
    def __init__(self):
        self.i = lax.axis_index("dp")
        self.j = lax.axis_index("mp")

    def bit(self, axis_bit):
        axis, b = axis_bit
        return self.j if axis == "mp" else lax.rem(self.i // 2**b, 2)

    def partner(self, flip):
        where = {}
        for axis, b in flip:
            if axis == "mp":
                where["mp"] = 1 - self.j
            else:
                step = 2**b - 2 ** (b + 1) * self.bit((axis, b))
                where["dp"] = where.get("dp", self.i) + step
        return where

    def number(self, bits, d=0):
        total = 0
        for m, e in enumerate(bits):
            bit = 1 - self.bit(e) if (d >> m) & 1 else self.bit(e)
            total = total + bit * 2**m
        return total


def remote(src, dst, send, recv, where):
    return pltpu.make_async_remote_copy(
        src_ref=src, dst_ref=dst, send_sem=send, recv_sem=recv, device_id=where, device_id_type=MESH
    )


class Exchange:
    def __init__(self, place, stages, send, recv):
        self.place, self.stages, self.send, self.recv = place, stages, send, recv
        self.before, self.first = [], []
        bits = copies = 0
        for stage in stages:
            self.before.append(bits)
            self.first.append(copies)
            bits += len(stage)
            copies += 2 ** len(stage) - 1

    def others(self, s):
        return range(1, 2 ** len(self.stages[s]))

    def flip(self, s, d):
        return [e for m, e in enumerate(self.stages[s]) if (d >> m) & 1]

    def link(self, s, d, src, dst):
        n = self.first[s] + d - 1
        return remote(
            src, dst, self.send.at[n], self.recv.at[n], self.place.partner(self.flip(s, d))
        )

    def start(self, s):
        for d in self.others(s):
            self.copy(s, d).start()

    def wait(self, s):
        for d in self.others(s):
            self.copy(s, d).wait_recv()

    def finish(self):
        for s in range(len(self.stages)):
            for d in self.others(s):
                self.copy(s, d).wait_send()


class Gather(Exchange):
    def __init__(self, place, stages, buf, send, recv):
        super().__init__(place, stages, send, recv)
        self.buf = buf
        self.slot = place.number([e for stage in stages for e in stage])

    def copy(self, s, d):
        size = 2 ** self.before[s]
        part = self.buf.at[pl.ds(self.slot - lax.rem(self.slot, size), size)]
        return self.link(s, d, part, part)


class Scatter(Exchange):
    def __init__(self, place, stages, total, out, came, send, recv):
        super().__init__(place, stages, send, recv)
        self.total, self.out, self.came = total, out, came
        self.top = len(stages) - 1
        self.own = place.number([e for stage in stages[:-1] for e in stage])

    def copy(self, s, d):
        size = 2 ** self.before[s]
        part = pl.ds(size * d, size)
        return self.link(s, d, self.out.at[part], self.came.at[part])

    def held(self, s, d=0):
        size = 2 ** self.before[s]
        base = self.own - lax.rem(self.own, size * 2 ** len(self.stages[s]))
        return pl.ds(base + size * self.place.number(self.stages[s], d), size)

    def start(self, s):
        if s < self.top:
            size = 2 ** self.before[s]
            for d in self.others(s):
                self.out[pl.ds(size * d, size)] = self.total[self.held(s, d)].astype(bf)
        super().start(s)

    def add(self, s):
        size = 2 ** self.before[s]
        self.wait(s)
        keep = pl.ds(0, size) if s == self.top else self.held(s)
        value = self.total[keep]
        for d in self.others(s):
            value = value + self.came[pl.ds(size * d, size)].astype(f32)
        self.total[keep] = value


class Sum(Exchange):
    def __init__(self, place, stages, bufs, send, recv):
        super().__init__(place, stages, send, recv)
        self.bufs = bufs

    def copy(self, s, d):
        part = self.bufs.at[s, self.place.number(self.stages[s])]
        return self.link(s, d, part, part)

    def begin(self, s, value):
        self.bufs[s, self.place.number(self.stages[s])] = value
        self.start(s)

    def total(self, s):
        self.wait(s)
        value = self.bufs[s, 0]
        for d in self.others(s):
            value = value + self.bufs[s, d]
        return value


def low_half(rows):
    return lax.broadcasted_iota(jnp.int32, (rows, 128), 1) < 64


def unpack(plan, groups, bufs, R, which):
    rows = plan.rows
    step = 16
    while step % rows and (step // 16) < 64:
        step += 16
    per = max(step // rows, 1)
    if (per * rows) % 16:
        raise ValueError("rows")
    first, last = (0, 3) if which == "A" else (3, 9)
    for m in range(plan.dp // per):
        tops, bottoms = [[], []], [[], []]
        for j in range(2):
            for f in range(first, last):
                g = next(n for n, e in enumerate(groups) if e[0] <= f < e[0] + e[1])
                lane = 128 * (f - groups[g][0])
                parts = [
                    bufs[g][slot_of(groups[g][2], m * per + n, j), :, lane : lane + 128].astype(f32)
                    for n in range(per)
                ]
                tops[j].append(jnp.concatenate([q[:rows] for q in parts], axis=0))
                bottoms[j].append(jnp.concatenate([q[rows : 2 * rows] for q in parts], axis=0))
        c0, c1 = tops[0] + bottoms[0], tops[1] + bottoms[1]
        size = per * rows
        lo = low_half(size)
        at = slice(m * size, (m + 1) * size)

        def put(ref, block, value):
            ref[at, 128 * block : 128 * block + 128] = value.astype(bf)

        if which == "A":
            for n in range(3):
                put(R.wqkv, 3 * n, c0[n])
                put(R.wqkv, 3 * n + 1, jnp.where(lo, c0[3 + n], c1[3 + n]))
                put(R.wqkv, 3 * n + 2, c1[n])
            put(R.wu, 10, jnp.where(lo, c1[3], c0[3]))
            put(R.wu, 11, jnp.where(lo, c1[4], c0[4]))
            put(R.wd, 10, jnp.where(lo, c1[5], c0[5]))
        else:
            put(R.wo, 0, c0[0])
            put(R.wo, 1, jnp.where(lo, c0[1], c1[1]))
            put(R.wo, 2, c1[0])
            put(R.wd, 11, jnp.where(lo, c1[1], c0[1]))
            for n in range(5):
                put(R.wu, n, c0[2 + n])
                put(R.wu, 5 + n, c1[2 + n])
                put(R.wd, n, c0[7 + n])
                put(R.wd, 5 + n, c1[7 + n])


def pack(plan, groups, scatters, R, core, which):
    rows = plan.rows
    lo = low_half(2 * rows)
    first, last = (0, 3) if which == "A" else (3, 9)
    for r in range(plan.dp // 2):
        at = slice(2 * r * rows, 2 * (r + 1) * rows)

        def get(ref, block):
            return ref[at, 128 * block : 128 * block + 128]

        def piece(j, n):
            if which == "A":
                if n < 3:
                    return get(R.Gqkv, 3 * n + 2 * j)
                own = get(R.Gqkv, 3 * (n - 3) + 1)
                fill = get(R.Gu, 7 + n) if n < 5 else get(R.Gd, 10)
            elif n == 0:
                return get(R.Go, 2 * j)
            elif n == 1:
                own, fill = get(R.Go, 1), get(R.Gd, 11)
            elif n < 7:
                return get(R.Gu, n - 2 + 5 * j)
            else:
                return get(R.Gd, n - 7 + 5 * j)
            return jnp.where(lo, own, fill) if j == 0 else jnp.where(lo, fill, own)

        for j in range(2):
            for f in range(first, last):
                g = next(n for n, e in enumerate(groups) if e[0] <= f < e[0] + e[1])
                lane = 128 * (f - groups[g][0])
                n = f - first
                top, bottom = piece(j, n), piece(j, n + last - first)
                even = jnp.concatenate([top[:rows], bottom[:rows]], axis=0)
                odd = jnp.concatenate([top[rows:], bottom[rows:]], axis=0)
                if plan.folded > 2 * rows:
                    none = jnp.zeros((plan.folded - 2 * rows, 128), f32)
                    even = jnp.concatenate([even, none], axis=0)
                    odd = jnp.concatenate([odd, none], axis=0)
                slot = slot_of(groups[g][2][:-1], 2 * r, j)
                half = plan.slots // 2
                scatters[g].out[half + slot, :, lane : lane + 128] = jnp.where(
                    core == 0, odd, even
                ).astype(bf)
                scatters[g].total[slot, :, lane : lane + 128] = jnp.where(core == 0, even, odd)


def own_chunk(plan, j, qkv, out_w, up, down):
    oT, dT = out_w, down

    def mix(own, fill):
        return jnp.where(
            j == 0,
            jnp.concatenate([own, fill], axis=1),
            jnp.concatenate([fill, own], axis=1),
        )

    part_a = [qkv[n, :, :128] for n in range(3)] + [
        mix(qkv[0, :, 128:192], up[:, 640:704]),
        mix(qkv[1, :, 128:192], up[:, 704:768]),
        mix(qkv[2, :, 128:192], dT[:, 640:704]),
    ]
    part_b = [oT[:, :128], mix(oT[:, 128:192], dT[:, 704:768])]
    part_b += [up[:, 128 * n : 128 * n + 128] for n in range(5)]
    part_b += [dT[:, 128 * n : 128 * n + 128] for n in range(5)]
    pad = plan.folded - 2 * plan.rows
    blocks = []
    for part in (part_a, part_b):
        half = len(part) // 2
        for n in range(half):
            rows = [part[n], part[n + half]]
            if pad:
                rows.append(jnp.zeros((pad, 128), f32))
            blocks.append(jnp.concatenate(rows, axis=0).astype(bf))
    return blocks


def wide_rows(plan, norm):
    values = norm[...].astype(bf).astype(f32)
    values = jnp.concatenate([values, jnp.zeros((2, 128 - plan.rows), f32)], axis=1)
    values = jnp.concatenate([values, jnp.zeros((6, 128), f32)], axis=0)
    return jnp.concatenate([values, jnp.zeros((8, D - 128), f32)], axis=1)


def layer_kernel(plan, *refs):
    it = iter(refs)
    take = lambda n: [next(it) for _ in range(n)]
    counts, inputs, out_grad = take(3)
    weights_in = take(5)
    bo_out, ig_out, grads_out, gn_out = take(4)
    weights = take(5)
    x, g, h1, qkv, p, o, dy, dqkv = take(8)
    wqkv, wo, wu, wd, Gqkv, Go, Gu, Gd, gn = take(9)
    bo, ig = take(2)
    ng, ns = len(plan.gather), len(plan.scatter)
    gbufs = take(ng)
    g_send, g_recv = take(2)
    totals, cames = take(ns), take(ns)
    outs = gbufs
    s_send, s_recv = take(2)
    gains_buf, gains_send, gains_recv = take(3)
    sums_buf, sums_send, sums_recv = take(3)
    load_sem, weight_sem, store_sem, x_send, x_recv = take(5)

    place = Place()
    i, j = place.i, place.j
    here = plan.here

    partners = plan.partners()
    barrier = pltpu.get_barrier_semaphore()
    for flip in partners:
        pl.semaphore_signal(barrier, inc=1, device_id=place.partner(flip), device_id_type=MESH)

    weight_loads = [
        pltpu.make_async_copy(src, dst, weight_sem.at[n])
        for n, (src, dst) in enumerate(zip(weights_in, weights))
    ]
    loads = []
    for n in range(here):
        for k, (src, dst) in enumerate(((inputs, x), (out_grad, g))):
            loads.append(
                pltpu.make_async_copy(src.at[j * here + n], dst.at[n], load_sem.at[k, n])
            )
    for c in weight_loads + loads:
        c.start()

    gathers = [
        Gather(place, stages, gbufs[n], g_send.at[n], g_recv.at[n])
        for n, (_, _, stages) in enumerate(plan.gather)
    ]
    scatters = [
        Scatter(place, stages, totals[n], outs[n], cames[n], s_send.at[n], s_recv.at[n])
        for n, (_, _, stages) in enumerate(plan.scatter)
    ]
    gains = Sum(place, plan.gains, gains_buf, gains_send, gains_recv)
    sums = Sum(place, plan.sums, sums_buf, sums_send, sums_recv)
    first = [c for c, e in zip(gathers, plan.gather) if e[0] < 3]
    second = [c for c, e in zip(gathers, plan.gather) if e[0] >= 3]
    late = [c for c, e in zip(scatters, plan.scatter) if e[0] < 3]
    early = [c for c, e in zip(scatters, plan.scatter) if e[0] >= 3]

    for c in weight_loads:
        c.wait()
    blocks = own_chunk(plan, j, *weights[:4])
    for c, (f, size, _) in zip(gathers, plan.gather):
        for n in range(size):
            c.buf[c.slot, :, 128 * n : 128 * n + 128] = blocks[f + n]
    mine = pltpu.roll(wide_rows(plan, weights[4]), i * plan.rows, 1)

    pl.semaphore_wait(barrier, len(partners))

    stages = len(plan.gather[0][2])
    for s in range(stages):
        for c in first:
            if s:
                c.wait(s - 1)
            c.start(s)
        if s < len(plan.gains):
            gains.begin(s, gains.total(s - 1) if s else mine)
        if 0 < s < stages - 1:
            for c in second:
                if s > 1:
                    c.wait(s - 2)
                c.start(s - 1)
        if s == 0:
            for ref in (Gqkv, Go, Gu, Gd, gn):
                ref[...] = jnp.zeros_like(ref)
    rounded = gains.total(len(plan.gains) - 1)
    R = types.SimpleNamespace(
        x=x, g=g, h1=h1, qkv=qkv, p=p, o=o, dy=dy, dqkv=dqkv, wqkv=wqkv, wo=wo, wu=wu, wd=wd,
        Gqkv=Gqkv, Go=Go, Gu=Gu, Gd=Gd, gn=gn, bo=bo, ig=ig,
    )
    R.g1 = rounded[0:1, :]
    R.g2 = rounded[1:2, :]
    for c in loads:
        c.wait()
    for c in first:
        c.wait(stages - 1)
    for c in second:
        c.wait(stages - 3)
        c.start(stages - 2)
    unpack(plan, plan.gather, gbufs, R, "A")

    def attend(n, carry):
        a1(n, R, counts[j * here + n])

        @pl.when(n == (here - 1) // 2)
        def _():
            for c in second:
                c.wait(stages - 2)
                c.start(stages - 1)

        return carry

    lax.fori_loop(0, here, attend, 0)
    for c in second:
        c.wait(stages - 1)
    unpack(plan, plan.gather, gbufs, R, "B")
    for c in gathers + [gains]:
        c.finish()

    def swap(n, k):
        ref, out = ((bo, bo_out), (ig, ig_out))[k]
        return (
            pltpu.make_async_copy(ref.at[n], out.at[j * here + n], store_sem.at[k, n]),
            remote(
                ref.at[n], out.at[j * here + n], x_send.at[k, n], x_recv.at[k, n], {"mp": 1 - j}
            ),
        )

    def feed(n, carry):
        a2(n, R)
        for c in swap(n, 0):
            c.start()
        return carry

    lax.fori_loop(0, here, feed, 0)

    core = place.bit(("dp", 0))
    pack(plan, plan.scatter, scatters, R, core, "B")
    top = len(plan.scatter[0][2]) - 1
    for c in early:
        c.start(top)

    def advance(group, s):
        for c in group:
            c.add(s)
            if s:
                c.start(s - 1)

    due = {0: top, here - 1: top - 1}

    def back(n, carry):
        cc(n, R)
        for c in swap(n, 1):
            c.start()
        for image, s in due.items():

            @pl.when(n == image)
            def _(s=s):
                advance(early, s)

        return carry

    lax.fori_loop(0, here, back, 0)

    pack(plan, plan.scatter, scatters, R, core, "A")
    for c in late:
        c.start(top)
    sums.begin(0, gn[...])
    s_early = top - 2
    for s in range(top, -1, -1):
        advance(late, s)
        step = top - s
        value = sums.total(step)
        if step + 1 < len(plan.sums):
            sums.begin(step + 1, value)
        if s_early >= 0:
            advance(early, s_early)
            s_early -= 1
    for c, (f, size, _) in zip(scatters, plan.scatter):
        grads_out[:, 128 * f : 128 * (f + size)] = c.total[c.own]
    gn_out[...] = value

    for c in scatters + [sums]:
        c.finish()
    for n in range(here):
        for k in range(2):
            own, away = swap(n, k)
            own.wait()
            away.wait()


def run_layer(plan, counts, inputs, out_grad, weights):
    here, slots, folded = plan.here, plan.slots, plan.folded
    vmem = pl.BlockSpec(memory_space=pltpu.VMEM)
    hbm = pl.BlockSpec(memory_space=pl.ANY)
    dma = pltpu.SemaphoreType.DMA
    out = jax.ShapeDtypeStruct
    ng, ns = len(plan.gather), len(plan.scatter)
    lanes_g = [128 * e[1] for e in plan.gather]
    assert [e[:2] for e in plan.gather] == [e[:2] for e in plan.scatter]
    lanes_s = [128 * e[1] for e in plan.scatter]
    copies_g = max(plan.copies(e[2]) for e in plan.gather)
    copies_s = max(plan.copies(e[2]) for e in plan.scatter)

    def sum_scratch(stages):
        return [
            pltpu.VMEM((len(stages), max(2 ** len(e) for e in stages), 8, D), f32),
            dma((plan.copies(stages),)),
            dma((plan.copies(stages),)),
        ]

    scratch = [pltpu.VMEM(w.shape, f32) for w in weights]
    scratch += [
        pltpu.VMEM((here, S, D), f32),
        pltpu.VMEM((here, S, D), f32),
        pltpu.VMEM((here, S, D), bf),
        pltpu.VMEM((here, S, 3 * D), bf),
        pltpu.VMEM((here, 3, S, 2 * S), f32),
        pltpu.VMEM((here, S, D), bf),
        pltpu.VMEM((here, S, D), f32),
        pltpu.VMEM((S, 3 * D), bf),
        pltpu.VMEM((D, 3 * D), bf),
        pltpu.VMEM((D, D), bf),
        pltpu.VMEM((D, 4 * D), bf),
        pltpu.VMEM((D, 4 * D), bf),
        pltpu.VMEM((D, 3 * D), f32),
        pltpu.VMEM((D, D), f32),
        pltpu.VMEM((D, 4 * D), f32),
        pltpu.VMEM((D, 4 * D), f32),
        pltpu.VMEM((8, D), f32),
        pltpu.VMEM((here, S, D), bf),
        pltpu.VMEM((here, S, D), bf),
    ]
    scratch += [pltpu.VMEM((slots, folded, n), bf) for n in lanes_g]
    scratch += [dma((ng, copies_g)), dma((ng, copies_g))]
    scratch += [pltpu.VMEM((slots // 2, folded, n), f32) for n in lanes_s]
    scratch += [pltpu.VMEM((slots, folded, n), bf) for n in lanes_s]
    scratch += [dma((ns, copies_s)), dma((ns, copies_s))]
    scratch += sum_scratch(plan.gains) + sum_scratch(plan.sums)
    scratch += [
        dma((2, here)),
        dma((len(weights),)),
        dma((2, here)),
        dma((2, here)),
        dma((2, here)),
    ]
    return pl.pallas_call(
        functools.partial(layer_kernel, plan),
        out_shape=[
            out(inputs.shape, bf),
            out(inputs.shape, bf),
            out((folded, 9 * 128), f32),
            out((8, D), f32),
        ],
        in_specs=[pl.BlockSpec(memory_space=pltpu.SMEM)] + [hbm] * (2 + len(weights)),
        out_specs=[hbm, hbm, vmem, vmem],
        scratch_shapes=scratch,
        compiler_params=pltpu.CompilerParams(
            collective_id=0, has_side_effects=True, vmem_limit_bytes=63 << 20
        ),
        name="layer",
    )(counts, inputs, out_grad, *weights)


def adamw_update(weight, gradient, first_moment, second_moment, step_rate, decay_rate):
    first_next = BETA_FIRST * first_moment + (1.0 - BETA_FIRST) * gradient
    second_next = BETA_SECOND * second_moment + (1.0 - BETA_SECOND) * gradient * gradient
    first_fixed = first_next / (1.0 - BETA_FIRST**STEP)
    second_fixed = second_next / (1.0 - BETA_SECOND**STEP)
    weight_next = weight - step_rate * (
        first_fixed / (jnp.sqrt(second_fixed) + EPS_ADAM) + decay_rate * weight
    )
    return (weight_next, first_next, second_next)


def own_gradients(plan, i, j, grads, sums):
    rows = plan.rows

    def block(f, lower):
        return grads[rows * lower : rows * (lower + 1), 128 * f : 128 * f + 128]

    part_a = [block(n, 0) for n in range(3)] + [block(n, 1) for n in range(3)]
    part_b = [block(3 + n, 0) for n in range(6)] + [block(3 + n, 1) for n in range(6)]

    def split(value):
        left, right = value[:, :64], value[:, 64:]
        return jnp.where(j == 0, left, right), jnp.where(j == 0, right, left)

    own, fill = zip(*[split(e) for e in part_a[3:] + part_b[1:2]])
    qkv = [jnp.concatenate([part_a[n], own[n]], axis=1) for n in range(3)]
    out_w = jnp.concatenate([part_b[0], own[3]], axis=1)
    up = jnp.concatenate(part_b[2:7] + [fill[0], fill[1]], axis=1)
    down = jnp.concatenate(part_b[7:12] + [fill[2], fill[3]], axis=1)
    norm = pltpu.roll(sums, D - i * rows, 1)[:2, :rows]
    return qkv, out_w, up, down, norm


RATES = (
    (RATE_QKV, DECAY_MATRIX),
    (RATE_OUT, DECAY_MATRIX),
    (RATE_UP, DECAY_MATRIX),
    (RATE_DOWN, DECAY_MATRIX),
    (RATE_NORM, 0.0),
)


def finish_kernel(plan, *refs):
    it = iter(refs)
    take = lambda n: [next(it) for _ in range(n)]
    bo_in, ig_in = take(2)
    small_in = take(17)
    bo_out, ig_out = take(2)
    small_out = take(20)
    low, full = take(2)
    small = take(17)
    results = take(20)
    in_sem, small_sem, out_sem, result_sem = take(4)
    i, j = lax.axis_index("dp"), lax.axis_index("mp")
    n_images = plan.images

    small_loads = [
        pltpu.make_async_copy(src, dst, small_sem.at[n])
        for n, (src, dst) in enumerate(zip(small_in, small))
    ]
    loads, stores = [], []
    for n in range(n_images):
        for k, (src, dst) in enumerate(((bo_in, bo_out), (ig_in, ig_out))):
            loads.append(pltpu.make_async_copy(src.at[n], low.at[k, n], in_sem.at[k, n]))
            stores.append(pltpu.make_async_copy(full.at[k, n], dst.at[n], out_sem.at[k, n]))
    half = len(loads) // 2
    for c in loads[:half] + small_loads + loads[half:]:
        c.start()

    def convert(n):
        k, image = n % 2, n // 2
        loads[n].wait()
        full[k, image] = low[k, image].astype(f32)
        stores[n].start()

    for n in range(half):
        convert(n)
    for c in small_loads:
        c.wait()
    gradients = own_gradients(plan, i, j, small[0][...], small[1][...])
    for n in range(5):
        weight, first, second = small[2 + n], small[7 + n], small[12 + n]
        for c in range(3) if n == 0 else [...]:
            gradient = gradients[0][c] if n == 0 else gradients[n]
            new = adamw_update(weight[c], gradient, first[c], second[c], *RATES[n])
            for k in range(3):
                results[5 * k + n][c] = new[k]
            results[15 + n][c] = gradient
    result_stores = [
        pltpu.make_async_copy(src, dst, result_sem.at[n])
        for n, (src, dst) in enumerate(zip(results, small_out))
    ]
    for c in result_stores:
        c.start()
    for n in range(half, len(loads)):
        convert(n)
    for c in stores + result_stores:
        c.wait()


def run_finish(plan, bo, ig, small):
    hbm = pl.BlockSpec(memory_space=pl.ANY)
    dma = pltpu.SemaphoreType.DMA
    out = jax.ShapeDtypeStruct
    weights = [e.shape for e in small[2:7]]
    return pl.pallas_call(
        functools.partial(finish_kernel, plan),
        out_shape=[out(bo.shape, f32), out(ig.shape, f32)] + [out(e, f32) for e in weights * 4],
        in_specs=[hbm] * 19,
        out_specs=[hbm] * 22,
        scratch_shapes=[pltpu.VMEM((2,) + bo.shape, bf), pltpu.VMEM((2,) + bo.shape, f32)]
        + [pltpu.VMEM(e.shape, f32) for e in small]
        + [pltpu.VMEM(e, f32) for e in weights * 4]
        + [dma((2, plan.images)), dma((17,)), dma((2, plan.images)), dma((20,))],
        compiler_params=pltpu.CompilerParams(vmem_limit_bytes=62 << 20),
        name="finish",
    )(bo, ig, *small)


def shards(dp, mp, inputs, out_grad, counts, *state):
    plan = Plan(dp, mp, state[2].shape[0], inputs.shape[0])
    turn = lambda arrays: tuple(e.T if n % 5 in (1, 3) else e for n, e in enumerate(arrays))
    state = turn(state)
    bo, ig, grads, sums = run_layer(plan, counts, inputs, out_grad, state[:5])
    bo, ig, *new = run_finish(plan, bo, ig, (grads, sums) + state)
    return (bo, ig) + turn(new)


def solution(mesh):
    stored = (
        P(None, "dp", "mp"),
        P("mp", "dp"),
        P("dp", "mp"),
        P("mp", "dp"),
        P(None, "dp"),
    )
    images = P("dp", None, None)
    return jax.shard_map(
        functools.partial(shards, mesh.shape["dp"], mesh.shape["mp"]),
        mesh=mesh,
        in_specs=(images, images, P("dp")) + stored * 3,
        out_specs=(images, images) + stored * 4,
        check_vma=False,
    )
```

```python
import functools
import types

import jax
import jax.numpy as jnp
from jax import lax
from jax.experimental import pallas as pl
from jax.experimental.pallas import tpu as pltpu
from jax.sharding import PartitionSpec as P

MESH = pl.DeviceIdType.MESH
bf = jnp.bfloat16
f32 = jnp.float32
S = 384
D = 384
NN=(((1,),(0,)),((),())); NT=(((1,),(1,)),((),())); TN=(((0,),(0,)),((),()))
def dot(a,b,dn=NN): return lax.dot_general(a,b,dn,preferred_element_type=f32)

def ln_stats(x):
    c = x - jnp.mean(x,axis=-1,keepdims=True)
    r = lax.rsqrt(jnp.mean(c*c,axis=-1,keepdims=True)+1e-6)
    return c*r, r

def gelu_parts(u):
    z = jnp.abs(u)*0.7071067811865476
    t = 1.0/(1.0+0.3275911*z)
    poly = t*(0.127414796 + t*(-0.142248368 + t*(0.7107068705 + t*(-0.7265760135 + t*0.5307027145))))
    E = jnp.exp(u*u*-0.5)
    h = poly*E
    phi = jnp.where(u>=0, 1.0-h, h)
    return phi, E*0.3989422804014327

def stack2(t, lo):
    z=jnp.zeros_like(t)
    return jnp.concatenate([jnp.where(lo,t,z),jnp.where(lo,z,t)],axis=0)

def unstackT(t):
    return jnp.concatenate([t[:64,:S],t[64:,S:]],axis=0).T

def a1(img, R, count):
    h1=(R.xh[img]*R.g1).astype(bf)
    R.h1[img]=h1
    for b in range(3):
        for m in range(3):
            c=m*384+128*b
            R.qkv[img,:,c:c+128]=dot(h1,R.wqkv[:,c:c+128]).astype(bf)
    lo=lax.broadcasted_iota(jnp.int32,(S,128),1)<64
    for b in range(3):
        q=R.qkv[img,:,128*b:128*b+128]*jnp.asarray(0.125,bf)
        k=R.qkv[img,:,384+128*b:512+128*b]
        v=R.qkv[img,:,768+128*b:896+128*b]
        q2=stack2(q,lo)
        s=dot(k,q2,NT)
        key=lax.broadcasted_iota(jnp.int32,(128,2*S),0)
        s=jnp.concatenate([s[:256],jnp.where(key<count,s[256:],-1e30)],axis=0)
        mx=jnp.max(s,axis=0,keepdims=True)
        e=jnp.exp(s-mx)
        p=e*(1.0/jnp.sum(e,axis=0,keepdims=True))
        p=p.astype(bf)
        R.p[img,b]=p
        oT=dot(v,p,TN)
        R.o[img,:,128*b:128*b+128]=unstackT(oT).astype(bf)

CH=512
def a2(img, R, between=lambda k: None):
    o=R.o[img]; x=R.x[img]; g=R.g[img]
    y1=x+dot(o,R.wo[...],NT)
    xh2,r2=ln_stats(y1)
    h2=(xh2*R.g2).astype(bf)
    dl=g.astype(bf)
    bo=y1; dh2=jnp.zeros((S,D),f32)
    for c0 in range(0,1536,CH):
        c=slice(c0,c0+CH)
        u=dot(h2,R.wu[:,c])
        da=dot(dl,R.wd[:,c])
        phi,ph=gelu_parts(u)
        a=(u*phi).astype(bf)
        du=(da*(phi+u*ph)).astype(bf)
        bo=bo+dot(a,R.wd[:,c],NT)
        dh2=dh2+dot(du,R.wu[:,c],NT)
        R.Gu[:,c]=R.Gu[:,c]+dot(h2,du,TN)
        R.Gd[:,c]=R.Gd[:,c]+dot(dl,a,TN)
        between(c0//CH)
    R.bo[img]=bo.astype(R.bo.dtype)
    e=dh2*R.g2
    m1=jnp.mean(e,axis=-1,keepdims=True)
    m2=jnp.mean(e*xh2,axis=-1,keepdims=True)
    dy=g+r2*(e-m1-xh2*m2)
    R.dy[img]=dy
    R.gn[1:2,:]=R.gn[1:2,:]+jnp.sum(dh2*xh2,axis=0,keepdims=True)
    R.Go[...]=R.Go[...]+dot(dy.astype(bf),o,TN)

def cc(img, slot, R):
    dm=R.dy[img].astype(bf)
    h1=R.h1[img]
    lo=lax.broadcasted_iota(jnp.int32,(S,128),1)<64
    for b in range(3):
        sl=slice(128*b,128*b+128)
        do=dot(dm,R.wo[:,sl]).astype(bf)
        do2=stack2(do,lo)
        q2=stack2(R.qkv[img,:,sl]*jnp.asarray(0.125,bf),lo)
        k=R.qkv[img,:,384+128*b:512+128*b]
        v=R.qkv[img,:,768+128*b:896+128*b]
        p=R.p[img,b]
        dv=dot(p,do2).astype(bf)
        p=p.astype(f32)
        dp=dot(v,do2,NT)
        inner=jnp.sum(p*dp,axis=0,keepdims=True)
        ds=(p*(dp-inner)).astype(bf)
        dk=dot(ds,q2).astype(bf)
        dq=(unstackT(dot(k,ds,TN))*0.125).astype(bf)
        R.dqkv[slot,:,sl]=dq; R.dqkv[slot,:,384+128*b:512+128*b]=dk; R.dqkv[slot,:,768+128*b:896+128*b]=dv
    R.Gqkv[...]=R.Gqkv[...]+dot(h1,R.dqkv[slot],TN)

def cc_out(img, slot, R):
    dh1=dot(R.dqkv[slot],R.wqkv[...],NT)
    xh1=R.xh[img]
    e=dh1*R.g1
    m1=jnp.mean(e,axis=-1,keepdims=True)
    m2=jnp.mean(e*xh1,axis=-1,keepdims=True)
    ig=R.dy[img]+R.r1[:,img:img+1]*(e-m1-xh1*m2)
    R.ig[img]=ig.astype(R.ig.dtype)
    R.gn[0:1,:]=R.gn[0:1,:]+jnp.sum(dh1*xh1,axis=0,keepdims=True)


STEP = 5
EPS_ADAM = 1e-08
BETA_FIRST = 0.5
BETA_SECOND = 0.5
DECAY_MATRIX = 0.01
RATE_QKV = 0.05
RATE_OUT = 0.2
RATE_UP = 0.05
RATE_DOWN = 0.03
RATE_NORM = 0.3


class Plan:
    def __init__(self, dp, mp, rows, images):
        assert mp == 2 and dp >= 8 and dp & (dp - 1) == 0
        self.dp, self.mp, self.rows = dp, mp, rows
        self.bits = dp.bit_length() - 1
        self.slots = dp * mp
        self.folded = -(-2 * rows // 16) * 16
        self.images = images
        self.here = images // mp
        high = [("dp", b) for b in range(2, self.bits)]
        x, y, core = ("mp", 0), ("dp", 1), ("dp", 0)
        split = lambda *stages: [e for e in stages if e]
        self.gather = [
            (0, 2, split(high, [x, y], [core])),
            (2, 1, split([x, y], high, [core])),
            (3, 2, split(high, [x, y], [core])),
            (5, 2, split(high, [x, y], [core])),
            (7, 2, split([x, y], high, [core])),
        ]
        self.scatter = [
            (0, 2, split([x], high, [y], [core])),
            (2, 1, split([x], [y], high, [core])),
            (3, 2, split([x], [y], high, [core])),
            (5, 2, split([x], high, [y], [core])),
            (7, 2, split([x], high, [y], [core])),
        ]
        self.gains = split(high, [y, core])
        self.sums = split([y, core], high, [x])

    def copies(self, stages):
        return sum(2 ** len(e) - 1 for e in stages)

    def partners(self):
        found = []
        for stages in [e[2] for e in self.gather + self.scatter] + [self.gains, self.sums]:
            for stage in stages:
                for d in range(1, 2 ** len(stage)):
                    flip = sorted(e for m, e in enumerate(stage) if (d >> m) & 1)
                    if flip not in found:
                        found.append(flip)
        return found


def slot_of(stages, i, j):
    total = 0
    for t, (axis, b) in enumerate(e for stage in stages for e in stage):
        bit = j if axis == "mp" else (i // 2**b) % 2
        total = total + bit * 2**t
    return total


class Place:
    def __init__(self):
        self.i = lax.axis_index("dp")
        self.j = lax.axis_index("mp")

    def bit(self, axis_bit):
        axis, b = axis_bit
        return self.j if axis == "mp" else lax.rem(self.i // 2**b, 2)

    def partner(self, flip):
        where = {}
        for axis, b in flip:
            if axis == "mp":
                where["mp"] = 1 - self.j
            else:
                step = 2**b - 2 ** (b + 1) * self.bit((axis, b))
                where["dp"] = where.get("dp", self.i) + step
        return where

    def number(self, bits, d=0):
        total = 0
        for m, e in enumerate(bits):
            bit = 1 - self.bit(e) if (d >> m) & 1 else self.bit(e)
            total = total + bit * 2**m
        return total


def remote(src, dst, send, recv, where):
    return pltpu.make_async_remote_copy(
        src_ref=src, dst_ref=dst, send_sem=send, recv_sem=recv, device_id=where, device_id_type=MESH
    )


class Exchange:
    def __init__(self, place, stages, send, recv):
        self.place, self.stages, self.send, self.recv = place, stages, send, recv
        self.before, self.first = [], []
        bits = copies = 0
        for stage in stages:
            self.before.append(bits)
            self.first.append(copies)
            bits += len(stage)
            copies += 2 ** len(stage) - 1

    def others(self, s):
        return range(1, 2 ** len(self.stages[s]))

    def flip(self, s, d):
        return [e for m, e in enumerate(self.stages[s]) if (d >> m) & 1]

    def link(self, s, d, src, dst):
        n = self.first[s] + d - 1
        return remote(
            src, dst, self.send.at[n], self.recv.at[n], self.place.partner(self.flip(s, d))
        )

    def start(self, s):
        for d in self.others(s):
            self.copy(s, d).start()

    def wait(self, s):
        for d in self.others(s):
            self.copy(s, d).wait_recv()

    def finish(self):
        for s in range(len(self.stages)):
            for d in self.others(s):
                self.copy(s, d).wait_send()


class Gather(Exchange):
    def __init__(self, place, stages, buf, send, recv):
        super().__init__(place, stages, send, recv)
        self.buf = buf
        self.slot = place.number([e for stage in stages for e in stage])

    def copy(self, s, d):
        size = 2 ** self.before[s]
        part = self.buf.at[pl.ds(self.slot - lax.rem(self.slot, size), size)]
        return self.link(s, d, part, part)


class Scatter(Exchange):
    def __init__(self, place, stages, total, out, came, send, recv):
        super().__init__(place, stages, send, recv)
        self.total, self.out, self.came = total, out, came
        self.top = len(stages) - 1
        self.own = place.number([e for stage in stages[:-1] for e in stage])

    def copy(self, s, d):
        size = 2 ** self.before[s]
        part = pl.ds(size * d, size)
        return self.link(s, d, self.out.at[part], self.came.at[part])

    def held(self, s, d=0):
        size = 2 ** self.before[s]
        base = self.own - lax.rem(self.own, size * 2 ** len(self.stages[s]))
        return pl.ds(base + size * self.place.number(self.stages[s], d), size)

    def start(self, s):
        if s < self.top:
            size = 2 ** self.before[s]
            for d in self.others(s):
                self.out[pl.ds(size * d, size)] = self.total[self.held(s, d)].astype(bf)
        super().start(s)

    def add(self, s):
        size = 2 ** self.before[s]
        self.wait(s)
        keep = pl.ds(0, size) if s == self.top else self.held(s)
        value = self.total[keep]
        for d in self.others(s):
            value = value + self.came[pl.ds(size * d, size)].astype(f32)
        self.total[keep] = value


class Sum(Exchange):
    def __init__(self, place, stages, bufs, send, recv):
        super().__init__(place, stages, send, recv)
        self.bufs = bufs

    def copy(self, s, d):
        part = self.bufs.at[s, self.place.number(self.stages[s])]
        return self.link(s, d, part, part)

    def begin(self, s, value):
        self.bufs[s, self.place.number(self.stages[s])] = value
        self.start(s)

    def total(self, s):
        self.wait(s)
        value = self.bufs[s, 0]
        for d in self.others(s):
            value = value + self.bufs[s, d]
        return value


def low_half(rows):
    return lax.broadcasted_iota(jnp.int32, (rows, 128), 1) < 64


def unpack(plan, groups, bufs, R, which):
    rows = plan.rows
    step = 16
    while step % rows and (step // 16) < 64:
        step += 16
    per = max(step // rows, 1)
    if (per * rows) % 16:
        raise ValueError("rows")
    first, last = (0, 3) if which == "A" else (3, 9)
    for m in range(plan.dp // per):
        tops, bottoms = [[], []], [[], []]
        for j in range(2):
            for f in range(first, last):
                g = next(n for n, e in enumerate(groups) if e[0] <= f < e[0] + e[1])
                lane = 128 * (f - groups[g][0])
                parts = [
                    bufs[g][slot_of(groups[g][2], m * per + n, j), :, lane : lane + 128].astype(f32)
                    for n in range(per)
                ]
                tops[j].append(jnp.concatenate([q[:rows] for q in parts], axis=0))
                bottoms[j].append(jnp.concatenate([q[rows : 2 * rows] for q in parts], axis=0))
        c0, c1 = tops[0] + bottoms[0], tops[1] + bottoms[1]
        size = per * rows
        lo = low_half(size)
        at = slice(m * size, (m + 1) * size)

        def put(ref, block, value):
            ref[at, 128 * block : 128 * block + 128] = value.astype(bf)

        if which == "A":
            for n in range(3):
                put(R.wqkv, 3 * n, c0[n])
                put(R.wqkv, 3 * n + 1, jnp.where(lo, c0[3 + n], c1[3 + n]))
                put(R.wqkv, 3 * n + 2, c1[n])
            put(R.wu, 10, jnp.where(lo, c1[3], c0[3]))
            put(R.wu, 11, jnp.where(lo, c1[4], c0[4]))
            put(R.wd, 10, jnp.where(lo, c1[5], c0[5]))
        else:
            put(R.wo, 0, c0[5])
            put(R.wo, 1, jnp.where(lo, c0[11], c1[11]))
            put(R.wo, 2, c1[5])
            put(R.wd, 11, jnp.where(lo, c1[11], c0[11]))
            for n in range(5):
                for j, c in enumerate((c0, c1)):
                    put(R.wu, 2 * n + j, c[n])
                    put(R.wd, 2 * n + j, c[6 + n])


def pack(plan, group, scatter, R, core):
    rows = plan.rows
    lo = low_half(2 * rows)
    first, size, stages = group
    half = plan.slots // 2
    for r in range(plan.dp // 2):
        at = slice(2 * r * rows, 2 * (r + 1) * rows)

        def get(ref, block):
            return ref[at, 128 * block : 128 * block + 128]

        def mixed(j, own, fill):
            return jnp.where(lo, own, fill) if j == 0 else jnp.where(lo, fill, own)

        def pair(j, f):
            if f < 3:
                fill = get(R.Gu, 10 + f) if f < 2 else get(R.Gd, 10)
                return get(R.Gqkv, 3 * f + 2 * j), mixed(j, get(R.Gqkv, 3 * f + 1), fill)
            if f < 8:
                return get(R.Gu, 2 * (f - 3) + j), get(R.Gd, 2 * (f - 3) + j)
            return get(R.Go, 2 * j), mixed(j, get(R.Go, 1), get(R.Gd, 11))

        for j in range(2):
            slot = slot_of(stages[:-1], 2 * r, j)
            for n in range(size):
                lane = 128 * n
                top, bottom = pair(j, first + n)
                even = jnp.concatenate([top[:rows], bottom[:rows]], axis=0)
                odd = jnp.concatenate([top[rows:], bottom[rows:]], axis=0)
                if plan.folded > 2 * rows:
                    none = jnp.zeros((plan.folded - 2 * rows, 128), f32)
                    even = jnp.concatenate([even, none], axis=0)
                    odd = jnp.concatenate([odd, none], axis=0)
                scatter.out[half + slot, :, lane : lane + 128] = jnp.where(
                    core == 0, odd, even
                ).astype(bf)
                scatter.total[slot, :, lane : lane + 128] = jnp.where(core == 0, even, odd)


def own_chunk(plan, j, qkv, out_w, up, down):
    oT, dT = out_w, down

    def mix(own, fill):
        return jnp.where(
            j == 0,
            jnp.concatenate([own, fill], axis=1),
            jnp.concatenate([fill, own], axis=1),
        )

    part_a = [qkv[n, :, :128] for n in range(3)] + [
        mix(qkv[0, :, 128:192], up[:, 640:704]),
        mix(qkv[1, :, 128:192], up[:, 704:768]),
        mix(qkv[2, :, 128:192], dT[:, 640:704]),
    ]
    part_b = [up[:, 128 * n : 128 * n + 128] for n in range(5)] + [oT[:, :128]]
    part_b += [dT[:, 128 * n : 128 * n + 128] for n in range(5)]
    part_b += [mix(oT[:, 128:192], dT[:, 704:768])]
    pad = plan.folded - 2 * plan.rows
    blocks = []
    for part in (part_a, part_b):
        half = len(part) // 2
        for n in range(half):
            rows = [part[n], part[n + half]]
            if pad:
                rows.append(jnp.zeros((pad, 128), f32))
            blocks.append(jnp.concatenate(rows, axis=0).astype(bf))
    return blocks


def wide_rows(plan, norm):
    values = norm[...].astype(bf).astype(f32)
    values = jnp.concatenate([values, jnp.zeros((2, 128 - plan.rows), f32)], axis=1)
    values = jnp.concatenate([values, jnp.zeros((6, 128), f32)], axis=0)
    return jnp.concatenate([values, jnp.zeros((8, D - 128), f32)], axis=1)


def layer_kernel(plan, *refs):
    it = iter(refs)
    take = lambda n: [next(it) for _ in range(n)]
    counts, inputs, out_grad = take(3)
    weights_in = take(5)
    bo_out, ig_out, grads_out, gn_out = take(4)
    weights = take(5)
    x, g, h1, qkv, p, o, dqkv, xh, r1 = take(9)
    dy = x
    wqkv, wo, wu, wd, Gqkv, Go, Gu, Gd, gn = take(9)
    bo, ig = take(2)
    ng, ns = len(plan.gather), len(plan.scatter)
    gbufs = take(ng)
    g_send, g_recv = take(2)
    totals, cames = take(ns), take(ns)
    outs = gbufs
    s_send, s_recv = take(2)
    gains_buf, gains_send, gains_recv = take(3)
    sums_buf, sums_send, sums_recv = take(3)
    load_sem, weight_sem, store_sem, x_send, x_recv = take(5)

    place = Place()
    i, j = place.i, place.j
    here = plan.here

    partners = plan.partners()
    barrier = pltpu.get_barrier_semaphore()
    for flip in partners:
        pl.semaphore_signal(barrier, inc=1, device_id=place.partner(flip), device_id_type=MESH)

    weight_loads = [
        pltpu.make_async_copy(src, dst, weight_sem.at[n])
        for n, (src, dst) in enumerate(zip(weights_in, weights))
    ]
    loads = []
    for n in range(here):
        for k, (src, dst) in enumerate(((inputs, x), (out_grad, g))):
            loads.append(
                pltpu.make_async_copy(src.at[j * here + n], dst.at[n], load_sem.at[k, n])
            )
    for c in weight_loads + loads:
        c.start()

    gathers = [
        Gather(place, stages, gbufs[n], g_send.at[n], g_recv.at[n])
        for n, (_, _, stages) in enumerate(plan.gather)
    ]
    scatters = [
        Scatter(place, stages, totals[n], outs[n], cames[n], s_send.at[n], s_recv.at[n])
        for n, (_, _, stages) in enumerate(plan.scatter)
    ]
    gains = Sum(place, plan.gains, gains_buf, gains_send, gains_recv)
    sums = Sum(place, plan.sums, sums_buf, sums_send, sums_recv)

    for c in weight_loads:
        c.wait()
    blocks = own_chunk(plan, j, *weights[:4])
    for c, (f, size, _) in zip(gathers, plan.gather):
        for n in range(size):
            c.buf[c.slot, :, 128 * n : 128 * n + 128] = blocks[f + n]
    mine = pltpu.roll(wide_rows(plan, weights[4]), i * plan.rows, 1)

    pl.semaphore_wait(barrier, len(partners))

    ga, gx, gb, ge, gc = gathers
    gains.begin(0, mine)
    ga.start(0)
    gx.start(0)
    for ref in (Gqkv, Go, Gu, Gd, gn):
        ref[...] = jnp.zeros_like(ref)

    def step(c, s):
        c.wait(s)
        c.start(s + 1)

    def norm_rows(n):
        loads[2 * n].wait()
        xh[n], r1[:, n : n + 1] = ln_stats(x[n])

    step(gx, 0)
    gains.begin(1, gains.total(0))
    step(ga, 0)
    gb.start(0)
    ge.start(0)
    gc.start(0)
    for n in range(here // 2):
        norm_rows(n)
    step(ga, 1)
    for n in range(here // 2, here):
        norm_rows(n)
    rounded = gains.total(1)
    R = types.SimpleNamespace(
        x=x, g=g, h1=h1, qkv=qkv, p=p, o=o, dy=dy, dqkv=dqkv, wqkv=wqkv, wo=wo, wu=wu, wd=wd,
        Gqkv=Gqkv, Go=Go, Gu=Gu, Gd=Gd, gn=gn, bo=bo, ig=ig, xh=xh, r1=r1,
    )
    R.g1 = rounded[0:1, :]
    R.g2 = rounded[1:2, :]
    step(gx, 1)
    step(gc, 0)
    step(gb, 0)
    step(ge, 0)
    ga.wait(2)
    gx.wait(2)
    unpack(plan, plan.gather, gbufs, R, "A")
    def attend(n, carry):
        a1(n, R, counts[j * here + n])
        return carry

    lax.fori_loop(0, here - 1, attend, 0)
    step(gb, 1)
    step(ge, 1)
    step(gc, 1)
    a1(here - 1, R, counts[j * here + here - 1])
    for n in range(here):
        loads[2 * n + 1].wait()
    for c in (gb, ge, gc):
        c.wait(2)
    unpack(plan, plan.gather, gbufs, R, "B")
    for c in gathers + [gains]:
        c.finish()

    def swap(n, k):
        ref, out = ((bo, bo_out), (ig, ig_out))[k]
        return (
            pltpu.make_async_copy(ref.at[n], out.at[j * here + n], store_sem.at[k, n]),
            remote(
                ref.at[n], out.at[j * here + n], x_send.at[k, n], x_recv.at[k, n], {"mp": 1 - j}
            ),
        )

    def feed(n, carry):
        a2(n, R)
        for c in swap(n, 0):
            c.start()
        return carry

    lax.fori_loop(0, here - 1, feed, 0)

    core = place.bit(("dp", 0))
    top = len(plan.scatter[0][2]) - 1

    def leave(n):
        pack(plan, plan.scatter[n], scatters[n], R, core)
        scatters[n].start(top)

    def advance(c, s):
        c.add(s)
        if s:
            c.start(s - 1)

    sa, sx, sb, se, sc = scatters

    def between(k):
        if k == 0:
            leave(2)
        if k == 1:
            advance(sb, top)
            leave(3)

    a2(here - 1, R, between)
    for c in swap(here - 1, 0):
        c.start()
    advance(se, top)
    leave(4)

    def give(n):
        cc_out(n, n % 2, R)
        for c in swap(n, 1):
            c.start()

    for n in range(here):
        cc(n, n % 2, R)
        if n < here - 2:
            give(n)
        if n == 0:
            advance(sc, top)
        if n == 1:
            advance(se, top - 1)
        if n == 2:
            advance(sb, top - 1)
    leave(0)
    leave(1)
    advance(sc, top - 1)
    give(here - 2)
    advance(sa, top)
    advance(sx, top)
    give(here - 1)
    sums.begin(0, gn[...])
    advance(se, top - 2)
    advance(sb, top - 2)
    sums.begin(1, sums.total(0))
    advance(sa, top - 1)
    advance(sx, top - 1)
    advance(sc, top - 2)
    sums.begin(2, sums.total(1))
    advance(sa, top - 2)
    advance(sx, top - 2)
    for c in (sb, se, sc):
        advance(c, 0)
    value = sums.total(2)
    advance(sa, 0)
    advance(sx, 0)
    for c, (f, size, _) in zip(scatters, plan.scatter):
        grads_out[:, 128 * f : 128 * (f + size)] = c.total[c.own]
    gn_out[...] = value

    for c in scatters + [sums]:
        c.finish()
    for n in range(here):
        for k in range(2):
            own, away = swap(n, k)
            own.wait()
            away.wait()


def run_layer(plan, counts, inputs, out_grad, weights):
    here, slots, folded = plan.here, plan.slots, plan.folded
    vmem = pl.BlockSpec(memory_space=pltpu.VMEM)
    hbm = pl.BlockSpec(memory_space=pl.ANY)
    dma = pltpu.SemaphoreType.DMA
    out = jax.ShapeDtypeStruct
    ng, ns = len(plan.gather), len(plan.scatter)
    lanes_g = [128 * e[1] for e in plan.gather]
    assert [e[:2] for e in plan.gather] == [e[:2] for e in plan.scatter]
    lanes_s = [128 * e[1] for e in plan.scatter]
    copies_g = max(plan.copies(e[2]) for e in plan.gather)
    copies_s = max(plan.copies(e[2]) for e in plan.scatter)

    def sum_scratch(stages):
        return [
            pltpu.VMEM((len(stages), max(2 ** len(e) for e in stages), 8, D), f32),
            dma((plan.copies(stages),)),
            dma((plan.copies(stages),)),
        ]

    scratch = [pltpu.VMEM(w.shape, f32) for w in weights]
    scratch += [
        pltpu.VMEM((here, S, D), f32),
        pltpu.VMEM((here, S, D), f32),
        pltpu.VMEM((here, S, D), bf),
        pltpu.VMEM((here, S, 3 * D), bf),
        pltpu.VMEM((here, 3, S, 2 * S), bf),
        pltpu.VMEM((here, S, D), bf),
        pltpu.VMEM((2, S, 3 * D), bf),
        pltpu.VMEM((here, S, D), f32),
        pltpu.VMEM((S, 128), f32),
        pltpu.VMEM((D, 3 * D), bf),
        pltpu.VMEM((D, D), bf),
        pltpu.VMEM((D, 4 * D), bf),
        pltpu.VMEM((D, 4 * D), bf),
        pltpu.VMEM((D, 3 * D), f32),
        pltpu.VMEM((D, D), f32),
        pltpu.VMEM((D, 4 * D), f32),
        pltpu.VMEM((D, 4 * D), f32),
        pltpu.VMEM((8, D), f32),
        pltpu.VMEM((here, S, D), bf),
        pltpu.VMEM((here, S, D), bf),
    ]
    scratch += [pltpu.VMEM((slots, folded, n), bf) for n in lanes_g]
    scratch += [dma((ng, copies_g)), dma((ng, copies_g))]
    scratch += [pltpu.VMEM((slots // 2, folded, n), f32) for n in lanes_s]
    scratch += [pltpu.VMEM((slots, folded, n), bf) for n in lanes_s]
    scratch += [dma((ns, copies_s)), dma((ns, copies_s))]
    scratch += sum_scratch(plan.gains) + sum_scratch(plan.sums)
    scratch += [
        dma((2, here)),
        dma((len(weights),)),
        dma((2, here)),
        dma((2, here)),
        dma((2, here)),
    ]
    return pl.pallas_call(
        functools.partial(layer_kernel, plan),
        out_shape=[
            out(inputs.shape, bf),
            out(inputs.shape, bf),
            out((folded, 9 * 128), f32),
            out((8, D), f32),
        ],
        in_specs=[pl.BlockSpec(memory_space=pltpu.SMEM)] + [hbm] * (2 + len(weights)),
        out_specs=[hbm, hbm, vmem, vmem],
        scratch_shapes=scratch,
        compiler_params=pltpu.CompilerParams(
            collective_id=0, has_side_effects=True, vmem_limit_bytes=63 << 20
        ),
        name="layer",
    )(counts, inputs, out_grad, *weights)


def adamw_update(weight, gradient, first_moment, second_moment, step_rate, decay_rate):
    first_next = BETA_FIRST * first_moment + (1.0 - BETA_FIRST) * gradient
    second_next = BETA_SECOND * second_moment + (1.0 - BETA_SECOND) * gradient * gradient
    first_fixed = first_next / (1.0 - BETA_FIRST**STEP)
    second_fixed = second_next / (1.0 - BETA_SECOND**STEP)
    weight_next = weight - step_rate * (
        first_fixed / (jnp.sqrt(second_fixed) + EPS_ADAM) + decay_rate * weight
    )
    return (weight_next, first_next, second_next)


def own_gradients(plan, i, j, grads, sums):
    rows = plan.rows

    def block(f, lower):
        return grads[rows * lower : rows * (lower + 1), 128 * f : 128 * f + 128]

    part_a = [block(n, 0) for n in range(3)] + [block(n, 1) for n in range(3)]
    part_b = [block(3 + n, 0) for n in range(6)] + [block(3 + n, 1) for n in range(6)]

    def split(value):
        left, right = value[:, :64], value[:, 64:]
        return jnp.where(j == 0, left, right), jnp.where(j == 0, right, left)

    own, fill = zip(*[split(e) for e in part_a[3:] + part_b[11:]])
    qkv = [jnp.concatenate([part_a[n], own[n]], axis=1) for n in range(3)]
    out_w = jnp.concatenate([part_b[5], own[3]], axis=1)
    up = jnp.concatenate(part_b[:5] + [fill[0], fill[1]], axis=1)
    down = jnp.concatenate(part_b[6:11] + [fill[2], fill[3]], axis=1)
    norm = pltpu.roll(sums, D - i * rows, 1)[:2, :rows]
    return qkv, out_w, up, down, norm


RATES = (
    (RATE_QKV, DECAY_MATRIX),
    (RATE_OUT, DECAY_MATRIX),
    (RATE_UP, DECAY_MATRIX),
    (RATE_DOWN, DECAY_MATRIX),
    (RATE_NORM, 0.0),
)


def finish_kernel(plan, *refs):
    it = iter(refs)
    take = lambda n: [next(it) for _ in range(n)]
    bo_in, ig_in = take(2)
    small_in = take(17)
    bo_out, ig_out = take(2)
    small_out = take(20)
    low, full = take(2)
    small = take(17)
    results = take(20)
    in_sem, small_sem, out_sem, result_sem = take(4)
    i, j = lax.axis_index("dp"), lax.axis_index("mp")
    n_images = plan.images

    small_loads = [
        pltpu.make_async_copy(src, dst, small_sem.at[n])
        for n, (src, dst) in enumerate(zip(small_in, small))
    ]
    loads, stores = [], []
    for n in range(n_images):
        for k, (src, dst) in enumerate(((bo_in, bo_out), (ig_in, ig_out))):
            loads.append(pltpu.make_async_copy(src.at[n], low.at[k, n], in_sem.at[k, n]))
            stores.append(pltpu.make_async_copy(full.at[k, n], dst.at[n], out_sem.at[k, n]))
    half = len(loads) // 2
    for c in loads[:half] + small_loads + loads[half:]:
        c.start()

    def convert(n):
        k, image = n % 2, n // 2
        loads[n].wait()
        full[k, image] = low[k, image].astype(f32)
        stores[n].start()

    for n in range(half):
        convert(n)
    for c in small_loads:
        c.wait()
    gradients = own_gradients(plan, i, j, small[0][...], small[1][...])
    for n in range(5):
        weight, first, second = small[2 + n], small[7 + n], small[12 + n]
        for c in range(3) if n == 0 else [...]:
            gradient = gradients[0][c] if n == 0 else gradients[n]
            new = adamw_update(weight[c], gradient, first[c], second[c], *RATES[n])
            for k in range(3):
                results[5 * k + n][c] = new[k]
            results[15 + n][c] = gradient
    result_stores = [
        pltpu.make_async_copy(src, dst, result_sem.at[n])
        for n, (src, dst) in enumerate(zip(results, small_out))
    ]
    for c in result_stores:
        c.start()
    for n in range(half, len(loads)):
        convert(n)
    for c in stores + result_stores:
        c.wait()


def run_finish(plan, bo, ig, small):
    hbm = pl.BlockSpec(memory_space=pl.ANY)
    dma = pltpu.SemaphoreType.DMA
    out = jax.ShapeDtypeStruct
    weights = [e.shape for e in small[2:7]]
    return pl.pallas_call(
        functools.partial(finish_kernel, plan),
        out_shape=[out(bo.shape, f32), out(ig.shape, f32)] + [out(e, f32) for e in weights * 4],
        in_specs=[hbm] * 19,
        out_specs=[hbm] * 22,
        scratch_shapes=[pltpu.VMEM((2,) + bo.shape, bf), pltpu.VMEM((2,) + bo.shape, f32)]
        + [pltpu.VMEM(e.shape, f32) for e in small]
        + [pltpu.VMEM(e, f32) for e in weights * 4]
        + [dma((2, plan.images)), dma((17,)), dma((2, plan.images)), dma((20,))],
        compiler_params=pltpu.CompilerParams(vmem_limit_bytes=62 << 20),
        name="finish",
    )(bo, ig, *small)


def shards(dp, mp, inputs, out_grad, counts, *state):
    plan = Plan(dp, mp, state[2].shape[0], inputs.shape[0])
    turn = lambda arrays: tuple(e.T if n % 5 in (1, 3) else e for n, e in enumerate(arrays))
    state = turn(state)
    bo, ig, grads, sums = run_layer(plan, counts, inputs, out_grad, state[:5])
    bo, ig, *new = run_finish(plan, bo, ig, (grads, sums) + state)
    return (bo, ig) + turn(new)


def solution(mesh):
    stored = (
        P(None, "dp", "mp"),
        P("mp", "dp"),
        P("dp", "mp"),
        P("mp", "dp"),
        P(None, "dp"),
    )
    images = P("dp", None, None)
    return jax.shard_map(
        functools.partial(shards, mesh.shape["dp"], mesh.shape["mp"]),
        mesh=mesh,
        in_specs=(images, images, P("dp")) + stored * 3,
        out_specs=(images, images) + stored * 4,
        check_vma=False,
    )
```

```python
import functools
import types

import jax
import jax.numpy as jnp
from jax import lax
from jax.experimental import pallas as pl
from jax.experimental.pallas import tpu as pltpu
from jax.sharding import PartitionSpec as P

MESH = pl.DeviceIdType.MESH
bf = jnp.bfloat16
f32 = jnp.float32
S = 384
D = 384
NN=(((1,),(0,)),((),())); NT=(((1,),(1,)),((),())); TN=(((0,),(0,)),((),()))
def dot(a,b,dn=NN): return lax.dot_general(a,b,dn,preferred_element_type=f32)

def ln_stats(x):
    c = x - jnp.mean(x,axis=-1,keepdims=True)
    r = lax.rsqrt(jnp.mean(c*c,axis=-1,keepdims=True)+1e-6)
    return c*r, r

def gelu_parts(u):
    z = jnp.abs(u)*0.7071067811865476
    t = 1.0/(1.0+0.3275911*z)
    poly = t*(0.127414796 + t*(-0.142248368 + t*(0.7107068705 + t*(-0.7265760135 + t*0.5307027145))))
    E = jnp.exp(u*u*-0.5)
    h = poly*E
    phi = jnp.where(u>=0, 1.0-h, h)
    return phi, E*0.3989422804014327

def stack2(t, lo):
    z=jnp.zeros_like(t)
    return jnp.concatenate([jnp.where(lo,t,z),jnp.where(lo,z,t)],axis=0)

def unstackT(t):
    return jnp.concatenate([t[:64,:S],t[64:,S:]],axis=0).T

def a1(img, R, count):
    h1=(R.xh[img]*R.g1).astype(bf)
    R.h1[img]=h1
    for b in range(3):
        for m in range(3):
            c=m*384+128*b
            R.qkv[img,:,c:c+128]=dot(h1,R.wqkv[:,c:c+128]).astype(bf)
    lo=lax.broadcasted_iota(jnp.int32,(S,128),1)<64
    for b in range(3):
        q=R.qkv[img,:,128*b:128*b+128]*jnp.asarray(0.125,bf)
        k=R.qkv[img,:,384+128*b:512+128*b]
        v=R.qkv[img,:,768+128*b:896+128*b]
        q2=stack2(q,lo)
        s=dot(k,q2,NT)
        key=lax.broadcasted_iota(jnp.int32,(128,2*S),0)
        s=jnp.concatenate([s[:256],jnp.where(key<count,s[256:],-1e30)],axis=0)
        mx=jnp.max(s,axis=0,keepdims=True)
        e=jnp.exp(s-mx)
        p=e*(1.0/jnp.sum(e,axis=0,keepdims=True))
        p=p.astype(bf)
        R.p[img,b]=p
        oT=dot(v,p,TN)
        R.o[img,:,128*b:128*b+128]=unstackT(oT).astype(bf)

CH=512
def a2(img, R, between=lambda k: None):
    o=R.o[img]; x=R.x[img]; g=R.g[img]
    y1=x+dot(o,R.wo[...],NT)
    xh2,r2=ln_stats(y1)
    h2=(xh2*R.g2).astype(bf)
    dl=g.astype(bf)
    bo=y1; dh2=jnp.zeros((S,D),f32)
    for c0 in range(0,1536,CH):
        c=slice(c0,c0+CH)
        u=dot(h2,R.wu[:,c])
        da=dot(dl,R.wd[:,c])
        phi,ph=gelu_parts(u)
        a=(u*phi).astype(bf)
        du=(da*(phi+u*ph)).astype(bf)
        bo=bo+dot(a,R.wd[:,c],NT)
        dh2=dh2+dot(du,R.wu[:,c],NT)
        R.Gu[:,c]=R.Gu[:,c]+dot(h2,du,TN)
        R.Gd[:,c]=R.Gd[:,c]+dot(dl,a,TN)
        between(c0//CH)
    R.bo[img]=bo.astype(R.bo.dtype)
    e=dh2*R.g2
    m1=jnp.mean(e,axis=-1,keepdims=True)
    m2=jnp.mean(e*xh2,axis=-1,keepdims=True)
    dy=g+r2*(e-m1-xh2*m2)
    R.dy[img]=dy
    R.gn[1:2,:]=R.gn[1:2,:]+jnp.sum(dh2*xh2,axis=0,keepdims=True)
    R.Go[...]=R.Go[...]+dot(dy.astype(bf),o,TN)

def cc(img, slot, R):
    dm=R.dy[img].astype(bf)
    h1=R.h1[img]
    lo=lax.broadcasted_iota(jnp.int32,(S,128),1)<64
    for b in range(3):
        sl=slice(128*b,128*b+128)
        do=dot(dm,R.wo[:,sl]).astype(bf)
        do2=stack2(do,lo)
        q2=stack2(R.qkv[img,:,sl]*jnp.asarray(0.125,bf),lo)
        k=R.qkv[img,:,384+128*b:512+128*b]
        v=R.qkv[img,:,768+128*b:896+128*b]
        p=R.p[img,b]
        dv=dot(p,do2).astype(bf)
        p=p.astype(f32)
        dp=dot(v,do2,NT)
        inner=jnp.sum(p*dp,axis=0,keepdims=True)
        ds=(p*(dp-inner)).astype(bf)
        dk=dot(ds,q2).astype(bf)
        dq=(unstackT(dot(k,ds,TN))*0.125).astype(bf)
        R.dqkv[slot,:,sl]=dq; R.dqkv[slot,:,384+128*b:512+128*b]=dk; R.dqkv[slot,:,768+128*b:896+128*b]=dv
    R.Gqkv[...]=R.Gqkv[...]+dot(h1,R.dqkv[slot],TN)

def cc_out(img, slot, R):
    dh1=dot(R.dqkv[slot],R.wqkv[...],NT)
    xh1=R.xh[img]
    e=dh1*R.g1
    m1=jnp.mean(e,axis=-1,keepdims=True)
    m2=jnp.mean(e*xh1,axis=-1,keepdims=True)
    ig=R.dy[img]+R.r1[:,img:img+1]*(e-m1-xh1*m2)
    R.ig[img]=ig.astype(R.ig.dtype)
    R.gn[0:1,:]=R.gn[0:1,:]+jnp.sum(dh1*xh1,axis=0,keepdims=True)


STEP = 5
EPS_ADAM = 1e-08
BETA_FIRST = 0.5
BETA_SECOND = 0.5
DECAY_MATRIX = 0.01
RATE_QKV = 0.05
RATE_OUT = 0.2
RATE_UP = 0.05
RATE_DOWN = 0.03
RATE_NORM = 0.3


class Plan:
    def __init__(self, dp, mp, rows, images):
        assert mp == 2 and dp >= 8 and dp & (dp - 1) == 0
        self.dp, self.mp, self.rows = dp, mp, rows
        self.bits = dp.bit_length() - 1
        self.slots = dp * mp
        self.folded = -(-2 * rows // 16) * 16
        self.images = images
        self.here = images // mp
        high = [("dp", b) for b in range(2, self.bits)]
        x, y, core = ("mp", 0), ("dp", 1), ("dp", 0)
        split = lambda *stages: [e for e in stages if e]
        self.gather = [
            (0, 2, split(high, [x, y], [core])),
            (2, 1, split([x, y], high, [core])),
            (3, 2, split(high, [x, y], [core])),
            (5, 2, split(high, [x, y], [core])),
            (7, 2, split([x, y], high, [core])),
        ]
        self.scatter = [
            (0, 2, split([x], high, [y], [core])),
            (2, 1, split([x], [y], high, [core])),
            (3, 2, split([x], [y], high, [core])),
            (5, 2, split([x], high, [y], [core])),
            (7, 2, split([x], high, [y], [core])),
        ]
        self.gains = split(high, [y, core])
        self.sums = split([y, core], high, [x])

    def copies(self, stages):
        return sum(2 ** len(e) - 1 for e in stages)

    def partners(self):
        found = []
        for stages in [e[2] for e in self.gather + self.scatter] + [self.gains, self.sums]:
            for stage in stages:
                for d in range(1, 2 ** len(stage)):
                    flip = sorted(e for m, e in enumerate(stage) if (d >> m) & 1)
                    if flip not in found:
                        found.append(flip)
        return found


def slot_of(stages, i, j):
    total = 0
    for t, (axis, b) in enumerate(e for stage in stages for e in stage):
        bit = j if axis == "mp" else (i // 2**b) % 2
        total = total + bit * 2**t
    return total


class Place:
    def __init__(self):
        self.i = lax.axis_index("dp")
        self.j = lax.axis_index("mp")

    def bit(self, axis_bit):
        axis, b = axis_bit
        return self.j if axis == "mp" else lax.rem(self.i // 2**b, 2)

    def partner(self, flip):
        where = {}
        for axis, b in flip:
            if axis == "mp":
                where["mp"] = 1 - self.j
            else:
                step = 2**b - 2 ** (b + 1) * self.bit((axis, b))
                where["dp"] = where.get("dp", self.i) + step
        return where

    def number(self, bits, d=0):
        total = 0
        for m, e in enumerate(bits):
            bit = 1 - self.bit(e) if (d >> m) & 1 else self.bit(e)
            total = total + bit * 2**m
        return total


def remote(src, dst, send, recv, where):
    return pltpu.make_async_remote_copy(
        src_ref=src, dst_ref=dst, send_sem=send, recv_sem=recv, device_id=where, device_id_type=MESH
    )


class Exchange:
    def __init__(self, place, stages, send, recv):
        self.place, self.stages, self.send, self.recv = place, stages, send, recv
        self.before, self.first = [], []
        bits = copies = 0
        for stage in stages:
            self.before.append(bits)
            self.first.append(copies)
            bits += len(stage)
            copies += 2 ** len(stage) - 1

    def others(self, s):
        return range(1, 2 ** len(self.stages[s]))

    def flip(self, s, d):
        return [e for m, e in enumerate(self.stages[s]) if (d >> m) & 1]

    def link(self, s, d, src, dst):
        n = self.first[s] + d - 1
        return remote(
            src, dst, self.send.at[n], self.recv.at[n], self.place.partner(self.flip(s, d))
        )

    def start(self, s):
        for d in self.others(s):
            self.copy(s, d).start()

    def wait(self, s):
        for d in self.others(s):
            self.copy(s, d).wait_recv()

    def finish(self):
        for s in range(len(self.stages)):
            for d in self.others(s):
                self.copy(s, d).wait_send()


class Gather(Exchange):
    def __init__(self, place, stages, buf, send, recv):
        super().__init__(place, stages, send, recv)
        self.buf = buf
        self.slot = place.number([e for stage in stages for e in stage])

    def copy(self, s, d):
        size = 2 ** self.before[s]
        part = self.buf.at[pl.ds(self.slot - lax.rem(self.slot, size), size)]
        return self.link(s, d, part, part)


class Scatter(Exchange):
    def __init__(self, place, stages, total, out, came, send, recv):
        super().__init__(place, stages, send, recv)
        self.total, self.out, self.came = total, out, came
        self.top = len(stages) - 1
        self.own = place.number([e for stage in stages[:-1] for e in stage])

    def copy(self, s, d):
        size = 2 ** self.before[s]
        part = pl.ds(size * d, size)
        return self.link(s, d, self.out.at[part], self.came.at[part])

    def held(self, s, d=0):
        size = 2 ** self.before[s]
        base = self.own - lax.rem(self.own, size * 2 ** len(self.stages[s]))
        return pl.ds(base + size * self.place.number(self.stages[s], d), size)

    def start(self, s):
        if s < self.top:
            size = 2 ** self.before[s]
            for d in self.others(s):
                self.out[pl.ds(size * d, size)] = self.total[self.held(s, d)].astype(bf)
        super().start(s)

    def add(self, s):
        size = 2 ** self.before[s]
        self.wait(s)
        keep = pl.ds(0, size) if s == self.top else self.held(s)
        value = self.total[keep]
        for d in self.others(s):
            value = value + self.came[pl.ds(size * d, size)].astype(f32)
        self.total[keep] = value


class Sum(Exchange):
    def __init__(self, place, stages, bufs, send, recv):
        super().__init__(place, stages, send, recv)
        self.bufs = bufs

    def copy(self, s, d):
        part = self.bufs.at[s, self.place.number(self.stages[s])]
        return self.link(s, d, part, part)

    def begin(self, s, value):
        self.bufs[s, self.place.number(self.stages[s])] = value
        self.start(s)

    def total(self, s):
        self.wait(s)
        value = self.bufs[s, 0]
        for d in self.others(s):
            value = value + self.bufs[s, d]
        return value


def low_half(rows):
    return lax.broadcasted_iota(jnp.int32, (rows, 128), 1) < 64


def unpack(plan, groups, bufs, R, which):
    rows = plan.rows
    step = 16
    while step % rows and (step // 16) < 64:
        step += 16
    per = max(step // rows, 1)
    if (per * rows) % 16:
        raise ValueError("rows")
    first, last = (0, 3) if which == "A" else (3, 9)
    for m in range(plan.dp // per):
        tops, bottoms = [[], []], [[], []]
        for j in range(2):
            for f in range(first, last):
                g = next(n for n, e in enumerate(groups) if e[0] <= f < e[0] + e[1])
                lane = 128 * (f - groups[g][0])
                parts = [
                    bufs[g][slot_of(groups[g][2], m * per + n, j), :, lane : lane + 128].astype(f32)
                    for n in range(per)
                ]
                tops[j].append(jnp.concatenate([q[:rows] for q in parts], axis=0))
                bottoms[j].append(jnp.concatenate([q[rows : 2 * rows] for q in parts], axis=0))
        c0, c1 = tops[0] + bottoms[0], tops[1] + bottoms[1]
        size = per * rows
        lo = low_half(size)
        at = slice(m * size, (m + 1) * size)

        def put(ref, block, value):
            ref[at, 128 * block : 128 * block + 128] = value.astype(bf)

        if which == "A":
            for n in range(3):
                put(R.wqkv, 3 * n, c0[n])
                put(R.wqkv, 3 * n + 1, jnp.where(lo, c0[3 + n], c1[3 + n]))
                put(R.wqkv, 3 * n + 2, c1[n])
            put(R.wu, 10, jnp.where(lo, c1[3], c0[3]))
            put(R.wu, 11, jnp.where(lo, c1[4], c0[4]))
            put(R.wd, 10, jnp.where(lo, c1[5], c0[5]))
        else:
            put(R.wo, 0, c0[5])
            put(R.wo, 1, jnp.where(lo, c0[11], c1[11]))
            put(R.wo, 2, c1[5])
            put(R.wd, 11, jnp.where(lo, c1[11], c0[11]))
            for n in range(5):
                for j, c in enumerate((c0, c1)):
                    put(R.wu, 2 * n + j, c[n])
                    put(R.wd, 2 * n + j, c[6 + n])


def pack(plan, group, scatter, R, core):
    rows = plan.rows
    lo = low_half(2 * rows)
    first, size, stages = group
    half = plan.slots // 2
    for r in range(plan.dp // 2):
        at = slice(2 * r * rows, 2 * (r + 1) * rows)

        def get(ref, block):
            return ref[at, 128 * block : 128 * block + 128]

        def mixed(j, own, fill):
            return jnp.where(lo, own, fill) if j == 0 else jnp.where(lo, fill, own)

        def pair(j, f):
            if f < 3:
                fill = get(R.Gu, 10 + f) if f < 2 else get(R.Gd, 10)
                return get(R.Gqkv, 3 * f + 2 * j), mixed(j, get(R.Gqkv, 3 * f + 1), fill)
            if f < 8:
                return get(R.Gu, 2 * (f - 3) + j), get(R.Gd, 2 * (f - 3) + j)
            return get(R.Go, 2 * j), mixed(j, get(R.Go, 1), get(R.Gd, 11))

        for j in range(2):
            slot = slot_of(stages[:-1], 2 * r, j)
            for n in range(size):
                lane = 128 * n
                top, bottom = pair(j, first + n)
                even = jnp.concatenate([top[:rows], bottom[:rows]], axis=0)
                odd = jnp.concatenate([top[rows:], bottom[rows:]], axis=0)
                if plan.folded > 2 * rows:
                    none = jnp.zeros((plan.folded - 2 * rows, 128), f32)
                    even = jnp.concatenate([even, none], axis=0)
                    odd = jnp.concatenate([odd, none], axis=0)
                scatter.out[half + slot, :, lane : lane + 128] = jnp.where(
                    core == 0, odd, even
                ).astype(bf)
                scatter.total[slot, :, lane : lane + 128] = jnp.where(core == 0, even, odd)


def own_chunk(plan, j, qkv, out_w, up, down):
    oT, dT = out_w, down

    def mix(own, fill):
        return jnp.where(
            j == 0,
            jnp.concatenate([own, fill], axis=1),
            jnp.concatenate([fill, own], axis=1),
        )

    part_a = [qkv[n, :, :128] for n in range(3)] + [
        mix(qkv[0, :, 128:192], up[:, 640:704]),
        mix(qkv[1, :, 128:192], up[:, 704:768]),
        mix(qkv[2, :, 128:192], dT[:, 640:704]),
    ]
    part_b = [up[:, 128 * n : 128 * n + 128] for n in range(5)] + [oT[:, :128]]
    part_b += [dT[:, 128 * n : 128 * n + 128] for n in range(5)]
    part_b += [mix(oT[:, 128:192], dT[:, 704:768])]
    pad = plan.folded - 2 * plan.rows
    blocks = []
    for part in (part_a, part_b):
        half = len(part) // 2
        for n in range(half):
            rows = [part[n], part[n + half]]
            if pad:
                rows.append(jnp.zeros((pad, 128), f32))
            blocks.append(jnp.concatenate(rows, axis=0).astype(bf))
    return blocks


def wide_rows(plan, norm):
    values = norm[...].astype(bf).astype(f32)
    values = jnp.concatenate([values, jnp.zeros((2, 128 - plan.rows), f32)], axis=1)
    values = jnp.concatenate([values, jnp.zeros((6, 128), f32)], axis=0)
    return jnp.concatenate([values, jnp.zeros((8, D - 128), f32)], axis=1)


def layer_kernel(plan, *refs):
    it = iter(refs)
    take = lambda n: [next(it) for _ in range(n)]
    counts, inputs, out_grad = take(3)
    weights_in = take(5)
    bo_out, ig_out, grads_out, gn_out = take(4)
    weights = take(5)
    x, g, h1, qkv, p, o, dqkv, xh, r1 = take(9)
    dy = x
    wqkv, wo, wu, wd, Gqkv, Go, Gu, Gd, gn = take(9)
    bo, ig = take(2)
    ng, ns = len(plan.gather), len(plan.scatter)
    gbufs = take(ng)
    g_send, g_recv = take(2)
    totals, cames = take(ns), take(ns)
    outs = gbufs
    s_send, s_recv = take(2)
    gains_buf, gains_send, gains_recv = take(3)
    sums_buf, sums_send, sums_recv = take(3)
    load_sem, weight_sem, store_sem, x_send, x_recv = take(5)

    place = Place()
    i, j = place.i, place.j
    here = plan.here

    partners = plan.partners()
    barrier = pltpu.get_barrier_semaphore()
    for flip in partners:
        pl.semaphore_signal(barrier, inc=1, device_id=place.partner(flip), device_id_type=MESH)

    weight_loads = [
        pltpu.make_async_copy(src, dst, weight_sem.at[n])
        for n, (src, dst) in enumerate(zip(weights_in, weights))
    ]
    loads = []
    for n in range(here):
        for k, (src, dst) in enumerate(((inputs, x), (out_grad, g))):
            loads.append(
                pltpu.make_async_copy(src.at[j * here + n], dst.at[n], load_sem.at[k, n])
            )
    for c in weight_loads + loads:
        c.start()

    gathers = [
        Gather(place, stages, gbufs[n], g_send.at[n], g_recv.at[n])
        for n, (_, _, stages) in enumerate(plan.gather)
    ]
    scatters = [
        Scatter(place, stages, totals[n], outs[n], cames[n], s_send.at[n], s_recv.at[n])
        for n, (_, _, stages) in enumerate(plan.scatter)
    ]
    gains = Sum(place, plan.gains, gains_buf, gains_send, gains_recv)
    sums = Sum(place, plan.sums, sums_buf, sums_send, sums_recv)

    for c in weight_loads:
        c.wait()
    blocks = own_chunk(plan, j, *weights[:4])
    for c, (f, size, _) in zip(gathers, plan.gather):
        for n in range(size):
            c.buf[c.slot, :, 128 * n : 128 * n + 128] = blocks[f + n]
    mine = pltpu.roll(wide_rows(plan, weights[4]), i * plan.rows, 1)

    pl.semaphore_wait(barrier, len(partners))

    ga, gx, gb, ge, gc = gathers
    gains.begin(0, mine)
    ga.start(0)
    gx.start(0)
    for ref in (Gqkv, Go, Gu, Gd, gn):
        ref[...] = jnp.zeros_like(ref)

    def step(c, s):
        c.wait(s)
        c.start(s + 1)

    def norm_rows(n):
        loads[2 * n].wait()
        xh[n], r1[:, n : n + 1] = ln_stats(x[n])

    step(gx, 0)
    gains.begin(1, gains.total(0))
    step(ga, 0)
    gb.start(0)
    ge.start(0)
    gc.start(0)
    for n in range(here // 2):
        norm_rows(n)
    step(ga, 1)
    for n in range(here // 2, here):
        norm_rows(n)
    rounded = gains.total(1)
    R = types.SimpleNamespace(
        x=x, g=g, h1=h1, qkv=qkv, p=p, o=o, dy=dy, dqkv=dqkv, wqkv=wqkv, wo=wo, wu=wu, wd=wd,
        Gqkv=Gqkv, Go=Go, Gu=Gu, Gd=Gd, gn=gn, bo=bo, ig=ig, xh=xh, r1=r1,
    )
    R.g1 = rounded[0:1, :]
    R.g2 = rounded[1:2, :]
    step(gx, 1)
    step(gc, 0)
    step(gb, 0)
    step(ge, 0)
    ga.wait(2)
    gx.wait(2)
    unpack(plan, plan.gather, gbufs, R, "A")
    def attend(n, carry):
        a1(n, R, counts[j * here + n])
        return carry

    lax.fori_loop(0, here - 1, attend, 0)
    step(gb, 1)
    step(ge, 1)
    step(gc, 1)
    a1(here - 1, R, counts[j * here + here - 1])
    for n in range(here):
        loads[2 * n + 1].wait()
    for c in (gb, ge, gc):
        c.wait(2)
    unpack(plan, plan.gather, gbufs, R, "B")
    for c in gathers + [gains]:
        c.finish()

    def swap(n, k):
        ref, out = ((bo, bo_out), (ig, ig_out))[k]
        return (
            pltpu.make_async_copy(ref.at[n], out.at[j * here + n], store_sem.at[k, n]),
            remote(
                ref.at[n], out.at[j * here + n], x_send.at[k, n], x_recv.at[k, n], {"mp": 1 - j}
            ),
        )

    def feed(n, carry):
        a2(n, R)
        for c in swap(n, 0):
            c.start()
        return carry

    lax.fori_loop(0, here - 1, feed, 0)

    core = place.bit(("dp", 0))
    top = len(plan.scatter[0][2]) - 1

    def leave(n):
        pack(plan, plan.scatter[n], scatters[n], R, core)
        scatters[n].start(top)

    def advance(c, s):
        c.add(s)
        if s:
            c.start(s - 1)

    sa, sx, sb, se, sc = scatters

    def between(k):
        if k == 0:
            leave(2)
        if k == 1:
            advance(sb, top)
            leave(3)

    a2(here - 1, R, between)
    for c in swap(here - 1, 0):
        c.start()
    advance(se, top)
    leave(4)

    def give(n):
        cc_out(n, n % 2, R)
        for c in swap(n, 1):
            c.start()

    for n in range(here):
        cc(n, n % 2, R)
        if n < here - 2:
            give(n)
        if n == 0:
            advance(sc, top)
        if n == 1:
            advance(se, top - 1)
        if n == 2:
            advance(sb, top - 1)
            advance(sc, top - 1)
    leave(0)
    leave(1)
    give(here - 2)
    advance(sa, top)
    advance(sx, top)
    give(here - 1)
    sums.begin(0, gn[...])
    advance(se, top - 2)
    advance(sb, top - 2)
    sums.begin(1, sums.total(0))
    advance(sa, top - 1)
    advance(sx, top - 1)
    advance(sc, top - 2)
    sums.begin(2, sums.total(1))
    advance(sa, top - 2)
    advance(sx, top - 2)
    for c in (sb, se, sc):
        advance(c, 0)
    value = sums.total(2)
    advance(sa, 0)
    advance(sx, 0)
    for c, (f, size, _) in zip(scatters, plan.scatter):
        grads_out[:, 128 * f : 128 * (f + size)] = c.total[c.own]
    gn_out[...] = value

    for c in scatters + [sums]:
        c.finish()
    for n in range(here):
        for k in range(2):
            own, away = swap(n, k)
            own.wait()
            away.wait()


def run_layer(plan, counts, inputs, out_grad, weights):
    here, slots, folded = plan.here, plan.slots, plan.folded
    vmem = pl.BlockSpec(memory_space=pltpu.VMEM)
    hbm = pl.BlockSpec(memory_space=pl.ANY)
    dma = pltpu.SemaphoreType.DMA
    out = jax.ShapeDtypeStruct
    ng, ns = len(plan.gather), len(plan.scatter)
    lanes_g = [128 * e[1] for e in plan.gather]
    assert [e[:2] for e in plan.gather] == [e[:2] for e in plan.scatter]
    lanes_s = [128 * e[1] for e in plan.scatter]
    copies_g = max(plan.copies(e[2]) for e in plan.gather)
    copies_s = max(plan.copies(e[2]) for e in plan.scatter)

    def sum_scratch(stages):
        return [
            pltpu.VMEM((len(stages), max(2 ** len(e) for e in stages), 8, D), f32),
            dma((plan.copies(stages),)),
            dma((plan.copies(stages),)),
        ]

    scratch = [pltpu.VMEM(w.shape, f32) for w in weights]
    scratch += [
        pltpu.VMEM((here, S, D), f32),
        pltpu.VMEM((here, S, D), f32),
        pltpu.VMEM((here, S, D), bf),
        pltpu.VMEM((here, S, 3 * D), bf),
        pltpu.VMEM((here, 3, S, 2 * S), bf),
        pltpu.VMEM((here, S, D), bf),
        pltpu.VMEM((2, S, 3 * D), bf),
        pltpu.VMEM((here, S, D), f32),
        pltpu.VMEM((S, 128), f32),
        pltpu.VMEM((D, 3 * D), bf),
        pltpu.VMEM((D, D), bf),
        pltpu.VMEM((D, 4 * D), bf),
        pltpu.VMEM((D, 4 * D), bf),
        pltpu.VMEM((D, 3 * D), f32),
        pltpu.VMEM((D, D), f32),
        pltpu.VMEM((D, 4 * D), f32),
        pltpu.VMEM((D, 4 * D), f32),
        pltpu.VMEM((8, D), f32),
        pltpu.VMEM((here, S, D), bf),
        pltpu.VMEM((here, S, D), bf),
    ]
    scratch += [pltpu.VMEM((slots, folded, n), bf) for n in lanes_g]
    scratch += [dma((ng, copies_g)), dma((ng, copies_g))]
    scratch += [pltpu.VMEM((slots // 2, folded, n), f32) for n in lanes_s]
    scratch += [pltpu.VMEM((slots, folded, n), bf) for n in lanes_s]
    scratch += [dma((ns, copies_s)), dma((ns, copies_s))]
    scratch += sum_scratch(plan.gains) + sum_scratch(plan.sums)
    scratch += [
        dma((2, here)),
        dma((len(weights),)),
        dma((2, here)),
        dma((2, here)),
        dma((2, here)),
    ]
    return pl.pallas_call(
        functools.partial(layer_kernel, plan),
        out_shape=[
            out(inputs.shape, bf),
            out(inputs.shape, bf),
            out((folded, 9 * 128), f32),
            out((8, D), f32),
        ],
        in_specs=[pl.BlockSpec(memory_space=pltpu.SMEM)] + [hbm] * (2 + len(weights)),
        out_specs=[hbm, hbm, vmem, vmem],
        scratch_shapes=scratch,
        compiler_params=pltpu.CompilerParams(
            collective_id=0, has_side_effects=True, vmem_limit_bytes=63 << 20
        ),
        name="layer",
    )(counts, inputs, out_grad, *weights)


def adamw_update(weight, gradient, first_moment, second_moment, step_rate, decay_rate):
    first_next = BETA_FIRST * first_moment + (1.0 - BETA_FIRST) * gradient
    second_next = BETA_SECOND * second_moment + (1.0 - BETA_SECOND) * gradient * gradient
    first_fixed = first_next / (1.0 - BETA_FIRST**STEP)
    second_fixed = second_next / (1.0 - BETA_SECOND**STEP)
    weight_next = weight - step_rate * (
        first_fixed / (jnp.sqrt(second_fixed) + EPS_ADAM) + decay_rate * weight
    )
    return (weight_next, first_next, second_next)


def own_gradients(plan, i, j, grads, sums):
    rows = plan.rows

    def block(f, lower):
        return grads[rows * lower : rows * (lower + 1), 128 * f : 128 * f + 128]

    part_a = [block(n, 0) for n in range(3)] + [block(n, 1) for n in range(3)]
    part_b = [block(3 + n, 0) for n in range(6)] + [block(3 + n, 1) for n in range(6)]

    def split(value):
        left, right = value[:, :64], value[:, 64:]
        return jnp.where(j == 0, left, right), jnp.where(j == 0, right, left)

    own, fill = zip(*[split(e) for e in part_a[3:] + part_b[11:]])
    qkv = [jnp.concatenate([part_a[n], own[n]], axis=1) for n in range(3)]
    out_w = jnp.concatenate([part_b[5], own[3]], axis=1)
    up = jnp.concatenate(part_b[:5] + [fill[0], fill[1]], axis=1)
    down = jnp.concatenate(part_b[6:11] + [fill[2], fill[3]], axis=1)
    norm = pltpu.roll(sums, D - i * rows, 1)[:2, :rows]
    return qkv, out_w, up, down, norm


RATES = (
    (RATE_QKV, DECAY_MATRIX),
    (RATE_OUT, DECAY_MATRIX),
    (RATE_UP, DECAY_MATRIX),
    (RATE_DOWN, DECAY_MATRIX),
    (RATE_NORM, 0.0),
)


def finish_kernel(plan, *refs):
    it = iter(refs)
    take = lambda n: [next(it) for _ in range(n)]
    bo_in, ig_in = take(2)
    small_in = take(17)
    bo_out, ig_out = take(2)
    small_out = take(20)
    low, full = take(2)
    small = take(17)
    results = take(20)
    in_sem, small_sem, out_sem, result_sem = take(4)
    i, j = lax.axis_index("dp"), lax.axis_index("mp")
    n_images = plan.images

    small_loads = [
        pltpu.make_async_copy(src, dst, small_sem.at[n])
        for n, (src, dst) in enumerate(zip(small_in, small))
    ]
    loads, stores = [], []
    for n in range(n_images // 2):
        at = pl.ds(2 * n, 2)
        for k, (src, dst) in enumerate(((bo_in, bo_out), (ig_in, ig_out))):
            loads.append(pltpu.make_async_copy(src.at[at], low.at[k, at], in_sem.at[k, n]))
            stores.append(pltpu.make_async_copy(full.at[k, at], dst.at[at], out_sem.at[k, n]))
    half = len(loads) // 2
    for c in loads[:half] + small_loads + loads[half:]:
        c.start()

    def convert(n):
        k, image = n % 2, n // 2
        loads[n].wait()
        at = pl.ds(2 * image, 2)
        full[k, at] = low[k, at].astype(f32)
        stores[n].start()

    for n in range(half):
        convert(n)
    for c in small_loads:
        c.wait()
    gradients = own_gradients(plan, i, j, small[0][...], small[1][...])
    for n in range(5):
        weight, first, second = small[2 + n], small[7 + n], small[12 + n]
        for c in range(3) if n == 0 else [...]:
            gradient = gradients[0][c] if n == 0 else gradients[n]
            new = adamw_update(weight[c], gradient, first[c], second[c], *RATES[n])
            for k in range(3):
                results[5 * k + n][c] = new[k]
            results[15 + n][c] = gradient
    result_stores = [
        pltpu.make_async_copy(src, dst, result_sem.at[n])
        for n, (src, dst) in enumerate(zip(results, small_out))
    ]
    for c in result_stores:
        c.start()
    for n in range(half, len(loads)):
        convert(n)
    for c in stores + result_stores:
        c.wait()


def run_finish(plan, bo, ig, small):
    hbm = pl.BlockSpec(memory_space=pl.ANY)
    dma = pltpu.SemaphoreType.DMA
    out = jax.ShapeDtypeStruct
    weights = [e.shape for e in small[2:7]]
    return pl.pallas_call(
        functools.partial(finish_kernel, plan),
        out_shape=[out(bo.shape, f32), out(ig.shape, f32)] + [out(e, f32) for e in weights * 4],
        in_specs=[hbm] * 19,
        out_specs=[hbm] * 22,
        scratch_shapes=[pltpu.VMEM((2,) + bo.shape, bf), pltpu.VMEM((2,) + bo.shape, f32)]
        + [pltpu.VMEM(e.shape, f32) for e in small]
        + [pltpu.VMEM(e, f32) for e in weights * 4]
        + [dma((2, plan.images)), dma((17,)), dma((2, plan.images)), dma((20,))],
        compiler_params=pltpu.CompilerParams(vmem_limit_bytes=62 << 20),
        name="finish",
    )(bo, ig, *small)


def shards(dp, mp, inputs, out_grad, counts, *state):
    plan = Plan(dp, mp, state[2].shape[0], inputs.shape[0])
    turn = lambda arrays: tuple(e.T if n % 5 in (1, 3) else e for n, e in enumerate(arrays))
    state = turn(state)
    bo, ig, grads, sums = run_layer(plan, counts, inputs, out_grad, state[:5])
    bo, ig, *new = run_finish(plan, bo, ig, (grads, sums) + state)
    return (bo, ig) + turn(new)


def solution(mesh):
    stored = (
        P(None, "dp", "mp"),
        P("mp", "dp"),
        P("dp", "mp"),
        P("mp", "dp"),
        P(None, "dp"),
    )
    images = P("dp", None, None)
    return jax.shard_map(
        functools.partial(shards, mesh.shape["dp"], mesh.shape["mp"]),
        mesh=mesh,
        in_specs=(images, images, P("dp")) + stored * 3,
        out_specs=(images, images) + stored * 4,
        check_vma=False,
    )
```
